512 devices in a mesh: band: 16 (over z), region: 32 (over y, x, core).
Axes of the slice: x: 4, y: 4, z: 16, core: 2. Of those that a mesh axis runs over, the one named last changes fastest.
Arguments:
- values: float32 [131072, 128], P(('band', 'region')), may hold values from -9 to 9
- coords: float32 [2, 131072], P(None, ('band', 'region')), may hold values from 0 to 2
- neighbours: int32 [1024, 256], P(('band', 'region')), may hold values from 0 to 131071, as said below
- log_params: float32 [3], replicated, may hold values from -0.5 to 0.5
Outputs:
- grad_values: float32 [131072, 128], P(('band', 'region'))
- grad_params: float32 [3], replicated
The draws below stay inside these ranges and needn't reach their ends.
Inputs may be any that keep to these rules, and one draw needn't show every extreme that they name: `neighbours`: the 256 indices of a block are distinct and none lies in the block. 160 of them lie on other devices of the block's band; in band 0 the others lie on the block's own device; in other bands 64 lie on the own device and 32 among the last 64 points of the device of the band below with the same region index. The blocks of one device use at most 11 distinct points of any other device of their band, in at most 22 entries, and both bounds are reached for some device pair of every device.
All inputs are finite; a program needn't handle non-finite values.
Results may differ from the reference program's by a relative error of at most 0.0003.
Values sent between devices are 32-bit elements; how exact they have to be, the bound alone decides.
A program may use at most 64 MiB of HBM per device.

```python
import jax
import jax.numpy as jnp
from jax import lax

B = 128
M = 256
REPS = 128
BLK_DEV = 2
P_DEV = 256
RIM = 64
M_LOC = 64
M_RIM = 32
HALF = 80
POOL = 160
CAP_U = 11
POINTS = 131072
BLOCKS = 1024
N_BAND = 16
N_REGION = 32


def draw_values(key, part):
    devices = N_BAND * N_REGION
    device = jnp.arange(POINTS) // P_DEV
    scale = 0.6 * 3.0 ** (device.astype(jnp.float32) / max(devices - 1, 1))
    key_base = jax.random.fold_in(key, 0)
    base = jnp.clip(jax.random.normal(key_base, (POINTS, REPS), jnp.float32), -5.0, 5.0)
    return scale[:, None] * base


def permute_rows(key, count, length):
    return jax.vmap(lambda sub_key: jax.random.permutation(sub_key, length))(jax.random.split(key, count))


def draw_neighbours(key, part):
    peers = N_REGION - 1
    devices = N_BAND * N_REGION

    def one_device(dev_key, device):
        keys = jax.random.split(dev_key, 7)
        band_id = device // N_REGION
        reg_id = device % N_REGION
        busy = jax.random.randint(keys[0], (), 1, 4)
        slot_pos = jnp.arange(POOL)
        first = busy * CAP_U
        rest = slot_pos - first
        peer_rank = jnp.where(slot_pos < first, slot_pos // CAP_U, busy + rest % (peers - busy))
        point_rank = jnp.where(slot_pos < first, slot_pos % CAP_U, rest // (peers - busy))
        shuffle_peers = jax.random.permutation(keys[1], peers)
        peer_reg = (reg_id + shuffle_peers[peer_rank] + 1) % N_REGION
        owner_perm = permute_rows(keys[2], N_REGION, P_DEV)
        far_points = (band_id * N_REGION + peer_reg) * P_DEV + owner_perm[peer_reg, point_rank]
        far_points = far_points[jax.random.permutation(keys[3], POOL)]
        segments = far_points.reshape(BLK_DEV, HALF)
        block_ids = jnp.arange(BLK_DEV)
        far_lists = jnp.concatenate([segments, segments[(block_ids - 1) % BLK_DEV]], axis=1)
        local_perm = permute_rows(keys[4], BLK_DEV, (BLK_DEV - 1) * B)[:, :M_LOC + M_RIM]
        local_pos = jnp.where(local_perm >= block_ids[:, None] * B, local_perm + B, local_perm)
        local_points = device * P_DEV + local_pos
        rim_perm = permute_rows(keys[5], BLK_DEV, RIM)[:, :M_RIM]
        rim_points = (device - N_REGION) * P_DEV + P_DEV - RIM + rim_perm
        edge_points = jnp.where(band_id > 0, rim_points, local_points[:, M_LOC:])
        lists = jnp.concatenate([local_points[:, :M_LOC], edge_points, far_lists], axis=1)
        order = permute_rows(keys[6], BLK_DEV, M)
        return jnp.take_along_axis(lists, order, axis=1)
    result = jax.vmap(one_device)(jax.random.split(key, devices), jnp.arange(devices))
    return result.reshape(devices * BLK_DEV, M).astype(jnp.int32)


def level_of(own_key, shape, cuts, low, largest):
    factor_of, own = 1.0, jax.random.fold_in(own_key, 6)
    for position, parts in cuts:
        heights = jnp.exp(jax.random.uniform(jax.random.fold_in(own, position), (parts,), jnp.float32, low / len(cuts), largest / len(cuts)))
        factor_of = factor_of * jnp.repeat(heights, shape[position] // parts).reshape([-1 if axis == position else 1 for axis in range(len(shape))])
    return factor_of


def setup_inputs(seed: int = 0) -> dict:
    key_list = jax.random.split(jax.random.key(seed), 5)
    return {
        "values": draw_values(jax.random.fold_in(key_list[4], 71), 0),
        "coords": jnp.clip(2.0 * jax.random.uniform(key_list[1], (2, POINTS), jnp.float32) ** level_of(key_list[1], (2, POINTS), ((1, 512),), -0.2, 0.2), 0.0, 2.0),
        "neighbours": draw_neighbours(jax.random.fold_in(key_list[4], 71), 0),
        "log_params": jnp.clip(jax.random.uniform(key_list[3], (3,), jnp.float32, -0.5, 0.5), -0.5, 0.5),
    }


def block_loglik(joint_rows, joint_coords, params):
    delta_x = joint_coords[:, 0][:, None] - joint_coords[:, 0][None, :]
    delta_y = joint_coords[:, 1][:, None] - joint_coords[:, 1][None, :]
    distance = jnp.sqrt(delta_x * delta_x + delta_y * delta_y)
    variance = jnp.exp(params[0])
    inverse_range = jnp.sqrt(3.0) * jnp.exp(-params[1])
    nugget = jnp.exp(params[2])
    scaled = inverse_range * distance
    order_n = joint_rows.shape[0]
    kernel = variance * (1.0 + scaled) * jnp.exp(-scaled) + nugget * jnp.eye(order_n, dtype=joint_rows.dtype)
    factor = jnp.linalg.cholesky(kernel)
    solved = jax.scipy.linalg.solve_triangular(factor, joint_rows, lower=True)
    tail_rows = solved[M:]
    log_diag = jnp.log(jnp.diagonal(factor)[M:])
    return -0.5 * jnp.sum(tail_rows * tail_rows) - joint_rows.shape[1] * jnp.sum(log_diag)

def reference(values, coords, neighbours, log_params):
    coord_rows = coords.T

    def step(carry, block_id):
        grad_sum, theta_sum = carry
        own_points = (block_id * B + jnp.arange(B)).astype(jnp.int32)
        joint_index = jnp.concatenate([neighbours[block_id].astype(jnp.int32), own_points])
        joint_rows = values[joint_index]
        joint_coords = coord_rows[joint_index]
        result, pullback = jax.vjp(lambda rows_in, params: block_loglik(rows_in, joint_coords, params), joint_rows, log_params)
        grad_rows, grad_theta = pullback(jnp.ones_like(result))
        return ((grad_sum.at[joint_index].add(grad_rows), theta_sum + grad_theta), None)
    start = (jnp.zeros_like(values), jnp.zeros_like(log_params))
    (grad_values, theta_total), _ = lax.scan(step, start, jnp.arange(BLOCKS).astype(jnp.int32))
    return (grad_values, theta_total / (POINTS * REPS))
```

```python
import functools

import jax
import jax.numpy as jnp
from jax import lax
from jax.experimental import pallas as pl
from jax.experimental.pallas import tpu as pltpu
from jax.sharding import PartitionSpec as P

MESH = pl.DeviceIdType.MESH
F32 = jnp.float32
BF16 = jnp.bfloat16
M = 256
RIM = 64
POOL = 160
STEPS_A = (0, 6, 1)
STEPS_S = (0, 6, 1)


def split(x, parts):
    out = []
    for _ in range(parts - 1):
        high = x.astype(BF16)
        out.append(high)
        x = x - high.astype(F32)
    out.append(x.astype(BF16))
    return out


def nn(a, b):
    return lax.dot_general(a, b, (((1,), (0,)), ((), ())), preferred_element_type=F32)


def nt(a, b):
    return lax.dot_general(a, b, (((1,), (1,)), ((), ())), preferred_element_type=F32)


def tn(a, b):
    return lax.dot_general(a, b, (((0,), (0,)), ((), ())), preferred_element_type=F32)


def one_pass(a, b):
    return nn(a.astype(BF16), b.astype(BF16))


def three_pass(a, b, dot=nn):
    a_high, a_low = split(a, 2)
    b_high, b_low = split(b, 2)
    return dot(a_high, b_high) + (dot(a_high, b_low) + dot(a_low, b_high))


def full(a, b):
    return jnp.dot(a, b, precision=lax.Precision.HIGHEST, preferred_element_type=F32)


def picked(dot, chosen, x, parts):
    return sum(dot(chosen, part) for part in reversed(split(x, parts)))


def iota(shape, dim):
    return lax.broadcasted_iota(jnp.int32, shape, dim)


def inverses(mats, refs, lowest, steps):
    n = mats[0].shape[0]
    eye = (iota((n, n), 0) == iota((n, n), 1)).astype(F32)
    lows = []
    for mat, ref in zip(mats, refs):
        sums = jnp.sum(jnp.abs(mat), axis=0, keepdims=True)
        top = jnp.max(sums, axis=1, keepdims=True) * 1.0001
        low = lowest / top
        scale = 2.0 / (top + lowest)
        ref[...] = (2.0 * scale) * eye - (scale * scale) * mat
        lows.append(4.0 * low / ((1.0 + low) * (1.0 + low)))

    def step(first, second, lows):
        later = []
        products = [first(mat, ref[...]) for mat, ref in zip(mats, refs)]
        for product, ref, low in zip(products, refs, lows):
            scale = 2.0 / (1.0 + low)
            held = ref[...]
            ref[...] = held + second(held, (2.0 * scale - 1.0) * eye - (scale * scale) * product)
            later.append(4.0 * low / ((1.0 + low) * (1.0 + low)))
        return later

    for count, first, second in zip(steps, (one_pass, three_pass, full), (one_pass, three_pass, three_pass)):
        if count:
            lows = lax.fori_loop(0, count, lambda i, l, f=first, s=second: tuple(step(f, s, l)), tuple(lows))
    return [ref[...] for ref in refs]


def kernel(
    n_band, n_reg, slots,
    values_ref, coords_ref, near_ref, params_ref,
    grad_ref, theta_ref,
    ask_out, ask_in, rows_out, rows_in, back_out, back_in,
    rim_out, rim_in, rimback_out, rimback_in,
    th_out, th_in, tb_out, tb_in,
    chosen_ref, spread_ref, sel_ref, kern_ref, shape_ref, slope_ref, inv_a0, inv_a1, inv_s0, inv_s1,
    send_sems, recv_sems,
):
    band, reg = lax.axis_index("band"), lax.axis_index("region")
    points, reps = values_ref.shape
    blocks, width = near_ref.shape
    length = points // blocks
    half = points // 2
    order_n = width + length
    rim_start = points - RIM

    def region_peer(i):
        return lax.rem(reg + i, n_reg)

    def band_peer(i):
        return lax.rem(band + i, n_band)

    barrier = pltpu.get_barrier_semaphore()

    def greet_region(i, c):
        pl.semaphore_signal(barrier, inc=1, device_id=(band, region_peer(i)), device_id_type=MESH)
        return c

    def greet_band(i, c):
        pl.semaphore_signal(barrier, inc=1, device_id=(band_peer(i), reg), device_id_type=MESH)
        return c

    lax.fori_loop(1, n_reg, greet_region, 0)
    lax.fori_loop(1, n_band, greet_band, 0)

    def to_peers(out, into, stage):
        def send(i, c):
            peer = region_peer(i)
            pltpu.make_async_remote_copy(
                src_ref=out.at[peer], dst_ref=into.at[reg],
                send_sem=send_sems.at[stage], recv_sem=recv_sems.at[stage],
                device_id=(band, peer), device_id_type=MESH,
            ).start()
            return c
        lax.fori_loop(1, n_reg, send, 0)

    def from_peers(out, into, stage):
        some = pl.ds(0, n_reg - 1)
        return pltpu.make_async_remote_copy(
            src_ref=out.at[some], dst_ref=into.at[some],
            send_sem=send_sems.at[stage], recv_sem=recv_sems.at[stage],
            device_id=(band, region_peer(1)), device_id_type=MESH,
        )

    near = near_ref[...]
    owner = near // points
    offset = near - owner * points
    owner_band = owner // n_reg
    owner_reg = owner - owner_band * n_reg
    is_rim = owner_band == band - 1
    is_own = jnp.logical_and(owner_band == band, owner_reg == reg)
    is_far = jnp.logical_and(owner_band == band, owner_reg != reg)
    far_row = jnp.where(is_far, owner_reg, -1)
    table_row = jnp.where(is_rim, n_reg, owner_reg)
    off_t = [(iota((points, width), 0) == offset[b : b + 1]).astype(BF16) for b in range(blocks)]
    far_t = [(iota((n_reg, width), 0) == far_row[b : b + 1]).astype(F32) for b in range(blocks)]
    counts = sum(nt(far_t[b].astype(BF16), off_t[b]) for b in range(blocks))
    mask = (counts > 0.5).astype(F32)
    below = (iota((points, points), 0) < iota((points, points), 1)).astype(BF16)
    rank = nn(mask.astype(BF16), below)

    x_row, y_row = coords_ref[0:1, :], coords_ref[1:2, :]
    ask_out[:, 0, :] = mask[:, :half]
    ask_out[:, 1, :] = mask[:, half:]
    for k, part in enumerate((x_row[:, :half], x_row[:, half:], y_row[:, :half], y_row[:, half:])):
        ask_out[:, 2 + k, :] = jnp.broadcast_to(part, (n_reg, half))
    ask_out[:, 6, :] = jnp.zeros((n_reg, half), F32)
    ask_out[:, 7, :] = jnp.zeros((n_reg, half), F32)
    rim_out[0:RIM, :] = values_ref[rim_start:, :]
    rim_out[RIM : RIM + 8, :] = jnp.concatenate(
        [x_row[:, half:], y_row[:, half:], jnp.zeros((6, half), F32)], axis=0
    )

    pl.semaphore_wait(barrier, n_reg + n_band - 2)
    to_peers(ask_out, ask_in, 0)
    rim_copy = pltpu.make_async_remote_copy(
        src_ref=rim_out, dst_ref=rim_in, send_sem=send_sems.at[4], recv_sem=recv_sems.at[4],
        device_id=(band_peer(1), reg), device_id_type=MESH,
    )
    rim_copy.start()
    ask_in[pl.ds(reg, 1)] = ask_out[pl.ds(reg, 1)]
    rows_in[pl.ds(reg, 1)] = jnp.zeros((1, slots, reps), F32)
    back_in[pl.ds(reg, 1)] = jnp.zeros((1, slots, reps), F32)

    rank_bf = rank.astype(BF16)
    index_rows = []
    for b in range(blocks):
        slot = jnp.sum(far_t[b] * nn(rank_bf, off_t[b]), axis=0, keepdims=True).astype(jnp.int32)
        far_index = points + RIM + owner_reg[b : b + 1] * slots + slot
        rim_index = points + offset[b : b + 1] - rim_start
        index_rows.append(
            jnp.where(is_own[b : b + 1], offset[b : b + 1], jnp.where(is_rim[b : b + 1], rim_index, far_index))
        )
    table = chosen_ref.shape[2]
    index_cols = jnp.concatenate(index_rows + [jnp.zeros((8 - blocks, width), jnp.int32)], axis=0).astype(F32).T
    for b in range(blocks):
        column = index_cols[:, b : b + 1].astype(jnp.int32)
        chosen_ref[b] = (iota((width, table), 1) == column).astype(BF16)
        spread_ref[b] = (iota((table, width), 0) == index_rows[b]).astype(BF16)

    from_peers(ask_out, ask_in, 0).wait_recv()
    rim_copy.wait_recv()

    wanted = jnp.concatenate([ask_in[:, 0, :], ask_in[:, 1, :]], axis=1)
    wanted_rank = nn(wanted.astype(BF16), below)
    slot_of = jnp.where(wanted > 0.5, wanted_rank, -1.0)
    sel = (
        jnp.broadcast_to(slot_of[:, None, :], (n_reg, slots, points))
        == iota((n_reg, slots, points), 1).astype(F32)
    )
    sel_ref[...] = sel.astype(F32).reshape(n_reg * slots, points).astype(BF16)
    rows_out[...] = picked(nn, sel_ref[...], values_ref[...], 3).reshape(n_reg, slots, reps)
    to_peers(rows_out, rows_in, 1)

    zero_half = jnp.zeros((1, half), F32)
    tables = []
    for k in range(2):
        peers = jnp.concatenate([ask_in[:, 2 + 2 * k, :], ask_in[:, 3 + 2 * k, :]], axis=1)
        rim_row = jnp.concatenate([zero_half, rim_in[RIM + k : RIM + k + 1, :]], axis=1)
        tables += [peers, rim_row, jnp.zeros((7, points), F32)]
    coord_table = jnp.concatenate(tables, axis=0)
    rows = n_reg + 8
    variance = jnp.exp(jnp.full((1, 1), params_ref[0], F32))
    inverse_range = jnp.sqrt(jnp.full((1, 1), 3.0, F32)) * jnp.exp(jnp.full((1, 1), -params_ref[1], F32))
    nugget = jnp.exp(jnp.full((1, 1), params_ref[2], F32))
    parts = split(coord_table, 3)
    for b in range(blocks):
        own_t = (iota((rows, width), 0) == table_row[b : b + 1]).astype(F32)
        found = sum(nn(part, off_t[b]) for part in reversed(parts))
        x_near = jnp.sum(own_t * found[:rows], axis=0, keepdims=True)
        y_near = jnp.sum(own_t * found[rows:], axis=0, keepdims=True)
        here = slice(b * length, (b + 1) * length)
        x_joint = jnp.concatenate([x_near, x_row[:, here]], axis=1)
        y_joint = jnp.concatenate([y_near, y_row[:, here]], axis=1)
        cols = jnp.concatenate([x_joint, y_joint, jnp.zeros((6, order_n), F32)], axis=0).T
        delta_x = cols[:, 0:1] - x_joint
        delta_y = cols[:, 1:2] - y_joint
        scaled = inverse_range * jnp.sqrt(delta_x * delta_x + delta_y * delta_y)
        decayed = variance * jnp.exp(-scaled)
        shape_part = decayed + scaled * decayed
        shape_ref[b] = shape_part
        slope_ref[b] = scaled * scaled * decayed
        diagonal = iota((order_n, order_n), 0) == iota((order_n, order_n), 1)
        kern_ref[b] = jnp.where(diagonal, shape_part + nugget, shape_part)

    all_blocks = range(blocks)
    inv_a = inverses([kern_ref[b, :width, :width] for b in all_blocks], [inv_a0, inv_a1], nugget, STEPS_A)
    x_t = [full(kern_ref[b, width:, :width], inv_a[b]) for b in all_blocks]
    x_n = [full(inv_a[b], kern_ref[b, :width, width:]) for b in all_blocks]
    schur = [kern_ref[b, width:, width:] - full(x_t[b], kern_ref[b, :width, width:]) for b in all_blocks]
    inv_s = inverses(schur, [inv_s0, inv_s1], nugget, STEPS_S)

    from_peers(rows_out, rows_in, 1).wait_recv()
    pad = table - points - RIM - n_reg * slots
    value_table = jnp.concatenate(
        [values_ref[...], rim_in[0:RIM, :], rows_in[...].reshape(n_reg * slots, reps), jnp.zeros((pad, reps), F32)],
        axis=0,
    )
    value_parts = split(value_table, 3)
    heads, us, backs, spread = [], [], [], 0.0
    for b in all_blocks:
        y_near = sum(nn(chosen_ref[b], part) for part in reversed(value_parts))
        here = slice(b * length, (b + 1) * length)
        resid = values_ref[here, :] - full(x_t[b], y_near)
        u = full(inv_s[b], resid)
        back_head = full(x_n[b], u)
        heads.append(three_pass(inv_a[b], y_near))
        us.append(u)
        backs.append(back_head)
        spread = spread + picked(nn, spread_ref[b], back_head, 3)
    back_out[...] = spread[points + RIM : points + RIM + n_reg * slots].reshape(n_reg, slots, reps)
    to_peers(back_out, back_in, 2)
    rimback_out[...] = spread[points : points + RIM]
    rimback_copy = pltpu.make_async_remote_copy(
        src_ref=rimback_out, dst_ref=rimback_in, send_sem=send_sems.at[5], recv_sem=recv_sems.at[5],
        device_id=(band_peer(n_band - 1), reg), device_id_type=MESH,
    )
    rimback_copy.start()
    grad_ref[...] = spread[:points] - jnp.concatenate(us, axis=0)

    sums = [jnp.zeros((1, 1), F32)] * 3
    for b in all_blocks:
        u, head_back = us[b], -backs[b]
        back = jnp.concatenate([head_back, u], axis=0)
        left = jnp.concatenate([heads[b] + 0.5 * head_back, 0.5 * u], axis=0)
        v = jnp.concatenate(
            [-x_n[b], (iota((length, length), 0) == iota((length, length), 1)).astype(F32)], axis=0
        )
        vs = (-0.5 * reps) * jnp.concatenate([-three_pass(x_n[b], inv_s[b]), inv_s[b]], axis=0)
        left = jnp.concatenate([left, vs], axis=1)
        right = jnp.concatenate([back, v], axis=1)
        grad_kernel = three_pass(left, right, nt)
        total = lambda z: jnp.sum(jnp.sum(z, axis=0, keepdims=True), axis=1, keepdims=True)
        sums = [
            sums[0] + total(grad_kernel * shape_ref[b]),
            sums[1] + total(grad_kernel * slope_ref[b]),
            sums[2] + nugget * total(left * right),
        ]
    lane = iota((1, half), 1)
    mine = jnp.where(lane == 0, sums[0], jnp.where(lane == 1, sums[1], jnp.where(lane == 2, sums[2], 0.0)))
    th_out[...] = mine

    def send_region(i, c):
        pltpu.make_async_remote_copy(
            src_ref=th_out, dst_ref=th_in.at[reg], send_sem=send_sems.at[3], recv_sem=recv_sems.at[3],
            device_id=(band, region_peer(i)), device_id_type=MESH,
        ).start()
        return c

    lax.fori_loop(1, n_reg, send_region, 0)
    th_in[pl.ds(reg, 1)] = mine[None]
    from_theta = pltpu.make_async_remote_copy(
        src_ref=th_in.at[pl.ds(0, n_reg - 1)], dst_ref=th_in.at[pl.ds(0, n_reg - 1)],
        send_sem=send_sems.at[3], recv_sem=recv_sems.at[3],
        device_id=(band, region_peer(1)), device_id_type=MESH,
    )
    from_theta.wait_recv()
    band_sum = jnp.sum(th_in[...], axis=0)
    tb_out[...] = band_sum

    def send_band(i, c):
        pltpu.make_async_remote_copy(
            src_ref=tb_out, dst_ref=tb_in.at[band], send_sem=send_sems.at[6], recv_sem=recv_sems.at[6],
            device_id=(band_peer(i), reg), device_id_type=MESH,
        ).start()
        return c

    lax.fori_loop(1, n_band, send_band, 0)
    tb_in[pl.ds(band, 1)] = band_sum[None]

    from_peers(back_out, back_in, 2).wait_recv()
    returned = back_in[...].reshape(n_reg * slots, reps)
    grad_ref[...] += picked(tn, sel_ref[...], returned, 3)
    rimback_copy.wait_recv()
    grad_ref[rim_start:, :] += rimback_in[...]

    from_bands = pltpu.make_async_remote_copy(
        src_ref=tb_in.at[pl.ds(0, n_band - 1)], dst_ref=tb_in.at[pl.ds(0, n_band - 1)],
        send_sem=send_sems.at[6], recv_sem=recv_sems.at[6],
        device_id=(band_peer(1), reg), device_id_type=MESH,
    )
    from_bands.wait_recv()
    theta_ref[...] = jnp.sum(tb_in[...], axis=0) * (1.0 / (points * n_band * n_reg * reps))

    from_peers(ask_out, ask_in, 0).wait_send()
    from_peers(rows_out, rows_in, 1).wait_send()
    from_peers(back_out, back_in, 2).wait_send()
    from_theta.wait_send()
    from_bands.wait_send()
    rim_copy.wait_send()
    rimback_copy.wait_send()


def shards(n_band, n_reg, values, coords, neighbours, log_params):
    points, reps = values.shape
    blocks, width = neighbours.shape
    length = points // blocks
    order_n = width + length
    cap = (2 * POOL + n_reg - 2) // (n_reg - 1)
    slots = -(-cap // 16) * 16
    table = -(-(points + RIM + n_reg * slots) // 128) * 128
    half = points // 2
    vmem = lambda *shape: pltpu.VMEM(shape, F32)
    grad, theta = pl.pallas_call(
        functools.partial(kernel, n_band, n_reg, slots),
        out_shape=(jax.ShapeDtypeStruct((points, reps), F32), jax.ShapeDtypeStruct((1, half), F32)),
        in_specs=[pl.BlockSpec(memory_space=pltpu.VMEM)] * 3 + [pl.BlockSpec(memory_space=pltpu.SMEM)],
        out_specs=(pl.BlockSpec(memory_space=pltpu.VMEM), pl.BlockSpec(memory_space=pltpu.VMEM)),
        scratch_shapes=[
            vmem(n_reg, 8, half), vmem(n_reg, 8, half),
            vmem(n_reg, slots, reps), vmem(n_reg, slots, reps),
            vmem(n_reg, slots, reps), vmem(n_reg, slots, reps),
            vmem(RIM + 8, reps), vmem(RIM + 8, reps), vmem(RIM, reps), vmem(RIM, reps),
            vmem(1, half), vmem(n_reg, 1, half), vmem(1, half), vmem(n_band, 1, half),
            pltpu.VMEM((blocks, width, table), BF16), pltpu.VMEM((blocks, table, width), BF16),
            pltpu.VMEM((n_reg * slots, points), BF16),
            vmem(blocks, order_n, order_n), vmem(blocks, order_n, order_n), vmem(blocks, order_n, order_n),
            vmem(width, width), vmem(width, width), vmem(length, length), vmem(length, length),
            pltpu.SemaphoreType.DMA((7,)), pltpu.SemaphoreType.DMA((7,)),
        ],
        compiler_params=pltpu.CompilerParams(
            collective_id=0, has_side_effects=True, vmem_limit_bytes=48 * 1024 * 1024
        ),
    )(values, coords, neighbours, log_params)
    return grad, theta[0, :3]


def solution(mesh):
    placed = (
        P(("band", "region"), None),
        P(None, ("band", "region")),
        P(("band", "region"), None),
        P(),
    )
    return jax.shard_map(
        functools.partial(shards, mesh.shape["band"], mesh.shape["region"]),
        mesh=mesh,
        in_specs=placed,
        out_specs=(P(("band", "region"), None), P()),
        check_vma=False,
    )
```

```python
import functools

import jax
import jax.numpy as jnp
from jax import lax
from jax.experimental import pallas as pl
from jax.experimental.pallas import tpu as pltpu
from jax.sharding import PartitionSpec as P

MESH = pl.DeviceIdType.MESH
F32 = jnp.float32
BF16 = jnp.bfloat16
M = 256
RIM = 64
POOL = 160


def split(x, parts):
    out = []
    for _ in range(parts - 1):
        high = x.astype(BF16)
        out.append(high)
        x = x - high.astype(F32)
    out.append(x.astype(BF16))
    return out


def nn(a, b):
    return lax.dot_general(a, b, (((1,), (0,)), ((), ())), preferred_element_type=F32)


def nt(a, b):
    return lax.dot_general(a, b, (((1,), (1,)), ((), ())), preferred_element_type=F32)


def tn(a, b):
    return lax.dot_general(a, b, (((0,), (0,)), ((), ())), preferred_element_type=F32)


def three_pass(a, b, dot=nn):
    a_high, a_low = split(a, 2)
    b_high, b_low = split(b, 2)
    return dot(a_high, b_high) + (dot(a_high, b_low) + dot(a_low, b_high))


def full(a, b):
    return jnp.dot(a, b, precision=lax.Precision.HIGHEST, preferred_element_type=F32)


def picked(dot, chosen, x, parts):
    return sum(dot(chosen, part) for part in reversed(split(x, parts)))


def iota(shape, dim):
    return lax.broadcasted_iota(jnp.int32, shape, dim)


def inverses(mats, refs, lowest, carried):
    n = mats[0].shape[0]
    eye = (iota((n, n), 0) == iota((n, n), 1)).astype(F32)

    def factor_of(product, low):
        scale = 2.0 / (1.0 + low)
        return (2.0 * scale) * eye - (scale * scale) * product

    def raised(low):
        return 4.0 * low / ((1.0 + low) * (1.0 + low))

    lows, factors, starts = [], [], []
    for mat in mats:
        sums = jnp.sum(jnp.abs(mat), axis=0, keepdims=True)
        over = 1.0 / (jnp.max(sums, axis=1, keepdims=True) * 1.0001)
        low = lowest * over
        start = over * mat
        factor = factor_of(start, low)
        starts.append(start)
        factors.append(factor)
        lows.append(raised(low))
    products = [three_pass(start, factor) for start, factor in zip(starts, factors)]
    for mat, ref, factor, product in zip(mats, refs, factors, products):
        over = jnp.max(jnp.sum(jnp.abs(mat), axis=0, keepdims=True), axis=1, keepdims=True) * 1.0001
        ref[:n] = factor / over
        ref[n:] = product

    def step(i, lows):
        held = [ref[...] for ref in refs]
        factors = [factor_of(both[n:], low) for both, low in zip(held, lows)]
        both = [three_pass(x, factor) for x, factor in zip(held, factors)]
        for ref, x in zip(refs, both):
            ref[...] = x
        return tuple(raised(low) for low in lows)

    lows = lax.fori_loop(0, carried, step, tuple(lows))
    found = [ref[:n] for ref in refs]
    products = [three_pass(mat, x) for mat, x in zip(mats, found)]
    found = [three_pass(x, factor_of(product, low)) for x, product, low in zip(found, products, lows)]
    lows = [raised(low) for low in lows]
    products = [full(mat, x) for mat, x in zip(mats, found)]
    return [
        x + three_pass(x, factor_of(product, low) - eye) for x, product, low in zip(found, products, lows)
    ]


def kernel(
    n_band, n_reg, slots,
    values_hbm, coords_hbm, near_hbm, params_hbm,
    grad_ref, theta_ref,
    values_ref, coords_ref, near_ref, params_ref,
    place_in, ask_out, ask_in, rows_out, rows_in, back_out, back_in,
    rimplace_in, rim_in, rimback_out, rimback_in,
    th_out, th_in, tb_out, tb_in,
    chosen_ref, spread_ref, sel_ref, kern_ref, shape_ref, slope_ref, inv_a0, inv_a1, inv_s0, inv_s1,
    local_sems, send_sems, recv_sems, known_sems,
):
    band, reg = lax.axis_index("band"), lax.axis_index("region")
    points, reps = values_ref.shape
    blocks, width = near_ref.shape
    length = points // blocks
    half = points // 2
    order_n = width + length
    rim_start = points - RIM

    def region_peer(i):
        return lax.rem(reg + i, n_reg)

    def band_peer(i):
        return lax.rem(band + i, n_band)

    arrivals = [
        pltpu.make_async_copy(source, target, local_sems.at[k])
        for k, (source, target) in enumerate(
            [(coords_hbm, coords_ref), (near_hbm, near_ref), (values_hbm, values_ref), (params_hbm, params_ref)]
        )
    ]
    for copy in arrivals:
        copy.start()

    barrier = pltpu.get_barrier_semaphore()

    def greet_region(i, c):
        pl.semaphore_signal(barrier, inc=1, device_id=(band, region_peer(i)), device_id_type=MESH)
        return c

    for i in (1, n_band - 1):
        pl.semaphore_signal(barrier, inc=1, device_id=(band_peer(i), reg), device_id_type=MESH)
    lax.fori_loop(1, n_reg, greet_region, 0)

    rounds = []
    while 2 ** (len(rounds) + 1) <= n_band // 2:
        rounds.append(2 ** len(rounds))

    def tell(k):
        for side, by in enumerate((rounds[k], n_band - rounds[k])):
            pl.semaphore_signal(
                known_sems.at[k, side], inc=1, device_id=(band_peer(by), reg), device_id_type=MESH
            )

    def hear(k):
        for side in range(2):
            pl.semaphore_wait(known_sems.at[k, side], 1)

    def to_peers(source, into, stage):
        def send(i, c):
            peer = region_peer(i)
            pltpu.make_async_remote_copy(
                src_ref=source(peer), dst_ref=into.at[reg],
                send_sem=send_sems.at[stage], recv_sem=recv_sems.at[stage],
                device_id=(band, peer), device_id_type=MESH,
            ).start()
            return c
        lax.fori_loop(1, n_reg, send, 0)

    def from_peers(into, stage):
        some = pl.ds(0, n_reg - 1)
        return pltpu.make_async_remote_copy(
            src_ref=into.at[some], dst_ref=into.at[some],
            send_sem=send_sems.at[stage], recv_sem=recv_sems.at[stage],
            device_id=(band, region_peer(1)), device_id_type=MESH,
        )

    def up_band(source, into, stage, by):
        return pltpu.make_async_remote_copy(
            src_ref=source, dst_ref=into, send_sem=send_sems.at[stage], recv_sem=recv_sems.at[stage],
            device_id=(band_peer(by), reg), device_id_type=MESH,
        )

    arrivals[0].wait()
    pl.semaphore_wait(barrier, n_reg + 1)
    to_peers(lambda peer: coords_ref, place_in, 0)
    rimplace_copy = up_band(coords_ref.at[:, pl.ds(half, half)], rimplace_in, 7, 1)
    rimplace_copy.start()
    if rounds:
        tell(0)
    place_in[pl.ds(reg, 1)] = coords_ref[...][None]

    arrivals[1].wait()
    near = near_ref[...]
    owner = near // points
    offset = near - owner * points
    owner_band = owner // n_reg
    owner_reg = owner - owner_band * n_reg
    is_rim = owner_band == band - 1
    is_own = jnp.logical_and(owner_band == band, owner_reg == reg)
    is_far = jnp.logical_and(owner_band == band, owner_reg != reg)
    far_row = jnp.where(is_far, owner_reg, -1)
    table_row = jnp.where(is_rim, n_reg, owner_reg)
    off_t = [(iota((points, width), 0) == offset[b : b + 1]).astype(BF16) for b in range(blocks)]
    far_t = [(iota((n_reg, width), 0) == far_row[b : b + 1]).astype(F32) for b in range(blocks)]
    counts = sum(nt(far_t[b].astype(BF16), off_t[b]) for b in range(blocks))
    mask = (counts > 0.5).astype(F32)
    below = (iota((points, points), 0) < iota((points, points), 1)).astype(BF16)
    rank = nn(mask.astype(BF16), below)
    ask_out[:, 0, :] = mask[:, :half]
    ask_out[:, 1, :] = mask[:, half:]
    to_peers(lambda peer: ask_out.at[peer], ask_in, 1)
    arrivals[2].wait()
    rim_copy = up_band(values_ref.at[pl.ds(rim_start, RIM)], rim_in, 4, 1)
    rim_copy.start()
    ask_in[pl.ds(reg, 1)] = jnp.zeros((1, 2, half), F32)
    rows_in[pl.ds(reg, 1)] = jnp.zeros((1, slots, reps), F32)
    back_in[pl.ds(reg, 1)] = jnp.zeros((1, slots, reps), F32)

    rank_bf = rank.astype(BF16)
    index_rows = []
    for b in range(blocks):
        slot = jnp.sum(far_t[b] * nn(rank_bf, off_t[b]), axis=0, keepdims=True).astype(jnp.int32)
        far_index = points + RIM + owner_reg[b : b + 1] * slots + slot
        rim_index = points + offset[b : b + 1] - rim_start
        index_rows.append(
            jnp.where(is_own[b : b + 1], offset[b : b + 1], jnp.where(is_rim[b : b + 1], rim_index, far_index))
        )
    table = chosen_ref.shape[2]
    index_cols = jnp.concatenate(index_rows + [jnp.zeros((8 - blocks, width), jnp.int32)], axis=0).astype(F32).T
    for b in range(blocks):
        column = index_cols[:, b : b + 1].astype(jnp.int32)
        chosen_ref[b] = (iota((width, table), 1) == column).astype(BF16)
        spread_ref[b] = (iota((table, width), 0) == index_rows[b]).astype(BF16)

    arrivals[3].wait()
    from_peers(place_in, 0).wait_recv()
    rimplace_copy.wait_recv()
    if len(rounds) > 1:
        hear(0)
        tell(1)

    x_row, y_row = coords_ref[0:1, :], coords_ref[1:2, :]
    zero_half = jnp.zeros((1, half), F32)
    tables = []
    for k in range(2):
        rim_row = jnp.concatenate([zero_half, rimplace_in[k : k + 1, :]], axis=1)
        tables += [place_in[:, k, :], rim_row, jnp.zeros((7, points), F32)]
    coord_table = jnp.concatenate(tables, axis=0)
    rows = n_reg + 8
    variance = jnp.exp(jnp.full((1, 1), params_ref[0], F32))
    inverse_range = jnp.sqrt(jnp.full((1, 1), 3.0, F32)) * jnp.exp(jnp.full((1, 1), -params_ref[1], F32))
    nugget = jnp.exp(jnp.full((1, 1), params_ref[2], F32))
    parts = split(coord_table, 3)
    for b in range(blocks):
        own_t = (iota((rows, width), 0) == table_row[b : b + 1]).astype(F32)
        found = sum(nn(part, off_t[b]) for part in reversed(parts))
        x_near = jnp.sum(own_t * found[:rows], axis=0, keepdims=True)
        y_near = jnp.sum(own_t * found[rows:], axis=0, keepdims=True)
        here = slice(b * length, (b + 1) * length)
        x_joint = jnp.concatenate([x_near, x_row[:, here]], axis=1)
        y_joint = jnp.concatenate([y_near, y_row[:, here]], axis=1)
        cols = jnp.concatenate([x_joint, y_joint, jnp.zeros((6, order_n), F32)], axis=0).T
        delta_x = cols[:, 0:1] - x_joint
        delta_y = cols[:, 1:2] - y_joint
        scaled = inverse_range * jnp.sqrt(delta_x * delta_x + delta_y * delta_y)
        decayed = variance * jnp.exp(-scaled)
        shape_part = decayed + scaled * decayed
        shape_ref[b] = shape_part
        slope_ref[b] = scaled * scaled * decayed
        diagonal = iota((order_n, order_n), 0) == iota((order_n, order_n), 1)
        kern_ref[b] = jnp.where(diagonal, shape_part + nugget, shape_part)

    from_peers(ask_in, 1).wait_recv()
    wanted = jnp.concatenate([ask_in[:, 0, :], ask_in[:, 1, :]], axis=1)
    wanted_rank = nn(wanted.astype(BF16), below)
    slot_of = jnp.where(wanted > 0.5, wanted_rank, -1.0)
    sel = (
        jnp.broadcast_to(slot_of[:, None, :], (n_reg, slots, points))
        == iota((n_reg, slots, points), 1).astype(F32)
    )
    sel_ref[...] = sel.astype(F32).reshape(n_reg * slots, points).astype(BF16)
    rows_out[...] = picked(nn, sel_ref[...], values_ref[...], 2).reshape(n_reg, slots, reps)
    to_peers(lambda peer: rows_out.at[peer], rows_in, 2)

    all_blocks = range(blocks)
    inv_a = inverses([kern_ref[b, :width, :width] for b in all_blocks], [inv_a0, inv_a1], nugget, 5)
    x_t = [full(kern_ref[b, width:, :width], inv_a[b]) for b in all_blocks]
    x_n = [x.T for x in x_t]
    schur = [kern_ref[b, width:, width:] - three_pass(x_t[b], kern_ref[b, :width, width:]) for b in all_blocks]
    if len(rounds) > 2:
        hear(1)
        tell(2)
    inv_s = inverses(schur, [inv_s0, inv_s1], nugget, 4)

    rim_copy.wait_recv()
    from_peers(rows_in, 2).wait_recv()
    pad = table - points - RIM - n_reg * slots
    value_table = jnp.concatenate(
        [values_ref[...], rim_in[...], rows_in[...].reshape(n_reg * slots, reps), jnp.zeros((pad, reps), F32)],
        axis=0,
    )
    value_parts = split(value_table, 2)
    near_rows = [sum(nn(chosen_ref[b], part) for part in reversed(value_parts)) for b in all_blocks]
    own_rows = [values_ref[b * length : (b + 1) * length, :] for b in all_blocks]
    resids = [own_rows[b] - three_pass(x_t[b], near_rows[b]) for b in all_blocks]
    heads = [three_pass(inv_a[b], near_rows[b]) for b in all_blocks]
    us = [three_pass(inv_s[b], resids[b]) for b in all_blocks]
    backs = [three_pass(x_n[b], us[b]) for b in all_blocks]

    sums = [jnp.zeros((1, 1), F32)] * 3
    for b in all_blocks:
        u, head_back = us[b], -backs[b]
        back = jnp.concatenate([head_back, u], axis=0)
        left = jnp.concatenate([heads[b] + 0.5 * head_back, 0.5 * u], axis=0)
        v = jnp.concatenate(
            [-x_n[b], (iota((length, length), 0) == iota((length, length), 1)).astype(F32)], axis=0
        )
        vs = (-0.5 * reps) * jnp.concatenate([-three_pass(x_n[b], inv_s[b]), inv_s[b]], axis=0)
        left = jnp.concatenate([left, vs], axis=1)
        right = jnp.concatenate([back, v], axis=1)
        grad_kernel = three_pass(left, right, nt)
        total = lambda z: jnp.sum(jnp.sum(z, axis=0, keepdims=True), axis=1, keepdims=True)
        sums = [
            sums[0] + total(grad_kernel * shape_ref[b]),
            sums[1] + total(grad_kernel * slope_ref[b]),
            sums[2] + nugget * total(left * right),
        ]
    lane = iota((1, half), 1)
    mine = jnp.where(lane == 0, sums[0], jnp.where(lane == 1, sums[1], jnp.where(lane == 2, sums[2], 0.0)))
    th_out[...] = mine
    to_peers(lambda peer: th_out, th_in, 5)
    th_in[pl.ds(reg, 1)] = mine[None]

    spread = sum(picked(nn, spread_ref[b], backs[b], 2) for b in all_blocks)
    back_out[...] = spread[points + RIM : points + RIM + n_reg * slots].reshape(n_reg, slots, reps)
    rimback_out[...] = spread[points : points + RIM]
    grad_ref[...] = spread[:points] - jnp.concatenate(us, axis=0)
    if rounds:
        hear(len(rounds) - 1)
    from_peers(th_in, 5).wait_recv()
    band_sum = jnp.sum(th_in[...], axis=0)
    tb_out[...] = band_sum

    def send_band(i, c):
        pltpu.make_async_remote_copy(
            src_ref=tb_out, dst_ref=tb_in.at[band], send_sem=send_sems.at[6], recv_sem=recv_sems.at[6],
            device_id=(band_peer(i), reg), device_id_type=MESH,
        ).start()
        return c

    lax.fori_loop(1, n_band, send_band, 0)
    tb_in[pl.ds(band, 1)] = band_sum[None]
    to_peers(lambda peer: back_out.at[peer], back_in, 3)
    rimback_copy = up_band(rimback_out, rimback_in, 8, n_band - 1)
    rimback_copy.start()

    rimback_copy.wait_recv()
    from_peers(back_in, 3).wait_recv()
    returned = back_in[...].reshape(n_reg * slots, reps)
    grad_ref[...] += picked(tn, sel_ref[...], returned, 2)
    grad_ref[rim_start:, :] += rimback_in[...]

    from_bands = pltpu.make_async_remote_copy(
        src_ref=tb_in.at[pl.ds(0, n_band - 1)], dst_ref=tb_in.at[pl.ds(0, n_band - 1)],
        send_sem=send_sems.at[6], recv_sem=recv_sems.at[6],
        device_id=(band_peer(1), reg), device_id_type=MESH,
    )
    from_bands.wait_recv()
    theta_ref[...] = jnp.sum(tb_in[...], axis=0) * (1.0 / (points * n_band * n_reg * reps))

    from_peers(place_in, 0).wait_send()
    from_peers(ask_in, 1).wait_send()
    from_peers(rows_in, 2).wait_send()
    from_peers(back_in, 3).wait_send()
    from_peers(th_in, 5).wait_send()
    from_bands.wait_send()
    rimplace_copy.wait_send()
    rim_copy.wait_send()
    rimback_copy.wait_send()


def shards(n_band, n_reg, values, coords, neighbours, log_params):
    points, reps = values.shape
    blocks, width = neighbours.shape
    length = points // blocks
    order_n = width + length
    cap = (2 * POOL + n_reg - 2) // (n_reg - 1)
    slots = -(-cap // 16) * 16
    table = -(-(points + RIM + n_reg * slots) // 128) * 128
    half = points // 2
    vmem = lambda *shape: pltpu.VMEM(shape, F32)
    grad, theta = pl.pallas_call(
        functools.partial(kernel, n_band, n_reg, slots),
        out_shape=(jax.ShapeDtypeStruct((points, reps), F32), jax.ShapeDtypeStruct((1, half), F32)),
        in_specs=[pl.BlockSpec(memory_space=pltpu.HBM)] * 4,
        out_specs=(pl.BlockSpec(memory_space=pltpu.VMEM), pl.BlockSpec(memory_space=pltpu.VMEM)),
        scratch_shapes=[
            vmem(points, reps), vmem(2, points), pltpu.VMEM((blocks, width), jnp.int32),
            pltpu.SMEM((3,), F32),
            vmem(n_reg, 2, points),
            vmem(n_reg, 2, half), vmem(n_reg, 2, half),
            vmem(n_reg, slots, reps), vmem(n_reg, slots, reps),
            vmem(n_reg, slots, reps), vmem(n_reg, slots, reps),
            vmem(2, half), vmem(RIM, reps), vmem(RIM, reps), vmem(RIM, reps),
            vmem(1, half), vmem(n_reg, 1, half), vmem(1, half), vmem(n_band, 1, half),
            pltpu.VMEM((blocks, width, table), BF16), pltpu.VMEM((blocks, table, width), BF16),
            pltpu.VMEM((n_reg * slots, points), BF16),
            vmem(blocks, order_n, order_n), vmem(blocks, order_n, order_n), vmem(blocks, order_n, order_n),
            vmem(2 * width, width), vmem(2 * width, width), vmem(2 * length, length), vmem(2 * length, length),
            pltpu.SemaphoreType.DMA((4,)), pltpu.SemaphoreType.DMA((9,)), pltpu.SemaphoreType.DMA((9,)),
            pltpu.SemaphoreType.REGULAR((4, 2)),
        ],
        compiler_params=pltpu.CompilerParams(
            collective_id=0, has_side_effects=True, vmem_limit_bytes=60 * 1024 * 1024
        ),
    )(values, coords, neighbours, log_params)
    return grad, theta[0, :3]


def solution(mesh):
    placed = (
        P(("band", "region"), None),
        P(None, ("band", "region")),
        P(("band", "region"), None),
        P(),
    )
    return jax.shard_map(
        functools.partial(shards, mesh.shape["band"], mesh.shape["region"]),
        mesh=mesh,
        in_specs=placed,
        out_specs=(P(("band", "region"), None), P()),
        check_vma=False,
    )
```

```python
import functools

import jax
import jax.numpy as jnp
from jax import lax
from jax.experimental import pallas as pl
from jax.experimental.pallas import tpu as pltpu
from jax.sharding import PartitionSpec as P

MESH = pl.DeviceIdType.MESH
F32 = jnp.float32
BF16 = jnp.bfloat16
M = 256
RIM = 64
POOL = 160


def split(x, parts):
    out = []
    for _ in range(parts - 1):
        high = x.astype(BF16)
        out.append(high)
        x = x - high.astype(F32)
    out.append(x.astype(BF16))
    return out


def nn(a, b):
    return lax.dot_general(a, b, (((1,), (0,)), ((), ())), preferred_element_type=F32)


def nt(a, b):
    return lax.dot_general(a, b, (((1,), (1,)), ((), ())), preferred_element_type=F32)


def tn(a, b):
    return lax.dot_general(a, b, (((0,), (0,)), ((), ())), preferred_element_type=F32)


def three_pass(a, b, dot=nn):
    a_high, a_low = split(a, 2)
    b_high, b_low = split(b, 2)
    return dot(a_high, b_high) + (dot(a_high, b_low) + dot(a_low, b_high))


def picked(dot, chosen, x, parts):
    return sum(dot(chosen, part) for part in reversed(split(x, parts)))


def iota(shape, dim):
    return lax.broadcasted_iota(jnp.int32, shape, dim)


def inverses(mats, refs, lowest, carried, last):
    n = mats[0].shape[0]
    eye = (iota((n, n), 0) == iota((n, n), 1)).astype(F32)

    def factor_of(product, low):
        scale = 2.0 / (1.0 + low)
        return (2.0 * scale) * eye - (scale * scale) * product

    def raised(low):
        return 4.0 * low / ((1.0 + low) * (1.0 + low))

    lows, factors, starts = [], [], []
    for mat in mats:
        sums = jnp.sum(jnp.abs(mat), axis=0, keepdims=True)
        over = 1.0 / (jnp.max(sums, axis=1, keepdims=True) * 1.0001)
        low = lowest * over
        start = over * mat
        factor = factor_of(start, low)
        starts.append(start)
        factors.append(factor)
        lows.append(raised(low))
    products = [three_pass(start, factor) for start, factor in zip(starts, factors)]
    for mat, ref, factor, product in zip(mats, refs, factors, products):
        over = jnp.max(jnp.sum(jnp.abs(mat), axis=0, keepdims=True), axis=1, keepdims=True) * 1.0001
        ref[:n] = factor / over
        ref[n:] = product

    def step(i, lows):
        held = [ref[...] for ref in refs]
        factors = [factor_of(both[n:], low) for both, low in zip(held, lows)]
        both = [three_pass(x, factor) for x, factor in zip(held, factors)]
        for ref, x in zip(refs, both):
            ref[...] = x
        return tuple(raised(low) for low in lows)

    lows = lax.fori_loop(0, carried, step, tuple(lows))
    found = [ref[:n] for ref in refs]
    products = [three_pass(mat, x) for mat, x in zip(mats, found)]
    found = [three_pass(x, factor_of(product, low)) for x, product, low in zip(found, products, lows)]
    if not last:
        return found
    lows = [raised(low) for low in lows]
    products = [three_pass(mat, x) for mat, x in zip(mats, found)]
    return [
        x + three_pass(x, factor_of(product, low) - eye) for x, product, low in zip(found, products, lows)
    ]


def kernel(
    n_band, n_reg, slots,
    values_hbm, coords_hbm, near_hbm, params_hbm,
    grad_ref, theta_ref,
    values_ref, coords_ref, near_ref, params_ref,
    place_in, ask_out, ask_in, rows_out, rows_in, back_out, back_in,
    rimplace_in, rim_in, rimback_out, rimback_in,
    th_out, th_in, tb_out, tb_in,
    chosen_ref, spread_ref, sel_ref, kern_ref, shape_ref, slope_ref, inv_a0, inv_a1, inv_s0, inv_s1,
    local_sems, send_sems, recv_sems, known_sems,
):
    band, reg = lax.axis_index("band"), lax.axis_index("region")
    points, reps = values_ref.shape
    blocks, width = near_ref.shape
    length = points // blocks
    half = points // 2
    order_n = width + length
    rim_start = points - RIM

    def turned(k, n):
        by = (k + 1) // 2
        return lax.rem(n // 2 + jnp.where(lax.rem(k, 2) == 0, by, n - by), n)

    side = 1
    while 2 * (2 * side) ** 2 <= n_reg:
        side *= 2
    tall = n_reg // (2 * side)

    def region_peer(i):
        k = i - 1
        y, x, core = reg // (2 * side), lax.rem(reg // 2, side), lax.rem(reg, 2)
        y = lax.rem(y + turned(k // (2 * side), tall), tall)
        x = lax.rem(x + turned(lax.rem(k // 2, side), side), side)
        core = lax.rem(core + 1 + lax.rem(k, 2), 2)
        return (y * side + x) * 2 + core

    def band_peer(i):
        return lax.rem(band + i, n_band)

    arrivals = [
        pltpu.make_async_copy(source, target, local_sems.at[k])
        for k, (source, target) in enumerate(
            [(coords_hbm, coords_ref), (near_hbm, near_ref), (values_hbm, values_ref), (params_hbm, params_ref)]
        )
    ]
    for copy in arrivals:
        copy.start()

    barrier = pltpu.get_barrier_semaphore()

    def greet_region(i, c):
        pl.semaphore_signal(barrier, inc=1, device_id=(band, region_peer(i)), device_id_type=MESH)
        return c

    for i in (1, n_band - 1):
        pl.semaphore_signal(barrier, inc=1, device_id=(band_peer(i), reg), device_id_type=MESH)
    lax.fori_loop(1, n_reg, greet_region, 0)

    rounds = []
    while 2 ** (len(rounds) + 1) <= n_band // 2:
        rounds.append(2 ** len(rounds))

    def tell(k):
        for side, by in enumerate((rounds[k], n_band - rounds[k])):
            pl.semaphore_signal(
                known_sems.at[k, side], inc=1, device_id=(band_peer(by), reg), device_id_type=MESH
            )

    def hear(k):
        for side in range(2):
            pl.semaphore_wait(known_sems.at[k, side], 1)

    def to_peers(source, into, stage):
        def send(i, c):
            peer = region_peer(i)
            pltpu.make_async_remote_copy(
                src_ref=source(peer), dst_ref=into.at[reg],
                send_sem=send_sems.at[stage], recv_sem=recv_sems.at[stage],
                device_id=(band, peer), device_id_type=MESH,
            ).start()
            return c
        lax.fori_loop(1, n_reg, send, 0)

    def from_peers(into, stage):
        some = pl.ds(0, n_reg - 1)
        return pltpu.make_async_remote_copy(
            src_ref=into.at[some], dst_ref=into.at[some],
            send_sem=send_sems.at[stage], recv_sem=recv_sems.at[stage],
            device_id=(band, region_peer(1)), device_id_type=MESH,
        )

    def up_band(source, into, stage, by):
        return pltpu.make_async_remote_copy(
            src_ref=source, dst_ref=into, send_sem=send_sems.at[stage], recv_sem=recv_sems.at[stage],
            device_id=(band_peer(by), reg), device_id_type=MESH,
        )

    arrivals[0].wait()
    pl.semaphore_wait(barrier, n_reg + 1)
    to_peers(lambda peer: coords_ref, place_in, 0)
    rimplace_copy = up_band(coords_ref.at[:, pl.ds(half, half)], rimplace_in, 7, 1)
    rimplace_copy.start()
    if rounds:
        tell(0)
    place_in[pl.ds(reg, 1)] = coords_ref[...][None]

    arrivals[1].wait()
    near = near_ref[...]
    owner = near // points
    offset = near - owner * points
    owner_band = owner // n_reg
    owner_reg = owner - owner_band * n_reg
    is_rim = owner_band == band - 1
    is_own = jnp.logical_and(owner_band == band, owner_reg == reg)
    is_far = jnp.logical_and(owner_band == band, owner_reg != reg)
    far_row = jnp.where(is_far, owner_reg, -1)
    table_row = jnp.where(is_rim, n_reg, owner_reg)
    off_t = [(iota((points, width), 0) == offset[b : b + 1]).astype(BF16) for b in range(blocks)]
    far_t = [(iota((n_reg, width), 0) == far_row[b : b + 1]).astype(F32) for b in range(blocks)]
    counts = sum(nt(far_t[b].astype(BF16), off_t[b]) for b in range(blocks))
    mask = (counts > 0.5).astype(F32)
    below = (iota((points, points), 0) < iota((points, points), 1)).astype(BF16)
    rank = nn(mask.astype(BF16), below)
    ask_out[:, 0, :] = mask[:, :half]
    ask_out[:, 1, :] = mask[:, half:]
    to_peers(lambda peer: ask_out.at[peer], ask_in, 1)
    arrivals[2].wait()
    rim_copy = up_band(values_ref.at[pl.ds(rim_start, RIM)], rim_in, 4, 1)
    rim_copy.start()
    ask_in[pl.ds(reg, 1)] = jnp.zeros((1, 2, half), F32)
    rows_in[pl.ds(reg, 1)] = jnp.zeros((1, slots, reps), F32)
    back_in[pl.ds(reg, 1)] = jnp.zeros((1, slots, reps), F32)

    rank_bf = rank.astype(BF16)
    index_rows = []
    for b in range(blocks):
        slot = jnp.sum(far_t[b] * nn(rank_bf, off_t[b]), axis=0, keepdims=True).astype(jnp.int32)
        far_index = points + RIM + owner_reg[b : b + 1] * slots + slot
        rim_index = points + offset[b : b + 1] - rim_start
        index_rows.append(
            jnp.where(is_own[b : b + 1], offset[b : b + 1], jnp.where(is_rim[b : b + 1], rim_index, far_index))
        )
    table = chosen_ref.shape[2]
    index_cols = jnp.concatenate(index_rows + [jnp.zeros((8 - blocks, width), jnp.int32)], axis=0).astype(F32).T
    for b in range(blocks):
        column = index_cols[:, b : b + 1].astype(jnp.int32)
        chosen_ref[b] = (iota((width, table), 1) == column).astype(BF16)
        spread_ref[b] = (iota((table, width), 0) == index_rows[b]).astype(BF16)

    arrivals[3].wait()
    from_peers(place_in, 0).wait_recv()
    rimplace_copy.wait_recv()
    if len(rounds) > 1:
        hear(0)
        tell(1)

    x_row, y_row = coords_ref[0:1, :], coords_ref[1:2, :]
    zero_half = jnp.zeros((1, half), F32)
    tables = []
    for k in range(2):
        rim_row = jnp.concatenate([zero_half, rimplace_in[k : k + 1, :]], axis=1)
        tables += [place_in[:, k, :], rim_row, jnp.zeros((7, points), F32)]
    coord_table = jnp.concatenate(tables, axis=0)
    rows = n_reg + 8
    variance = jnp.exp(jnp.full((1, 1), params_ref[0], F32))
    inverse_range = jnp.sqrt(jnp.full((1, 1), 3.0, F32)) * jnp.exp(jnp.full((1, 1), -params_ref[1], F32))
    nugget = jnp.exp(jnp.full((1, 1), params_ref[2], F32))
    parts = split(coord_table, 3)
    for b in range(blocks):
        own_t = (iota((rows, width), 0) == table_row[b : b + 1]).astype(F32)
        found = sum(nn(part, off_t[b]) for part in reversed(parts))
        x_near = jnp.sum(own_t * found[:rows], axis=0, keepdims=True)
        y_near = jnp.sum(own_t * found[rows:], axis=0, keepdims=True)
        here = slice(b * length, (b + 1) * length)
        x_joint = jnp.concatenate([x_near, x_row[:, here]], axis=1)
        y_joint = jnp.concatenate([y_near, y_row[:, here]], axis=1)
        cols = jnp.concatenate([x_joint, y_joint, jnp.zeros((6, order_n), F32)], axis=0).T
        delta_x = cols[:, 0:1] - x_joint
        delta_y = cols[:, 1:2] - y_joint
        scaled = inverse_range * jnp.sqrt(delta_x * delta_x + delta_y * delta_y)
        decayed = variance * jnp.exp(-scaled)
        shape_part = decayed + scaled * decayed
        shape_ref[b] = shape_part
        slope_ref[b] = scaled * scaled * decayed
        diagonal = iota((order_n, order_n), 0) == iota((order_n, order_n), 1)
        kern_ref[b] = jnp.where(diagonal, shape_part + nugget, shape_part)

    from_peers(ask_in, 1).wait_recv()
    wanted = jnp.concatenate([ask_in[:, 0, :], ask_in[:, 1, :]], axis=1)
    wanted_rank = nn(wanted.astype(BF16), below)
    slot_of = jnp.where(wanted > 0.5, wanted_rank, -1.0)
    sel = (
        jnp.broadcast_to(slot_of[:, None, :], (n_reg, slots, points))
        == iota((n_reg, slots, points), 1).astype(F32)
    )
    sel_ref[...] = sel.astype(F32).reshape(n_reg * slots, points).astype(BF16)
    rows_out[...] = picked(nn, sel_ref[...], values_ref[...], 2).reshape(n_reg, slots, reps)
    to_peers(lambda peer: rows_out.at[peer], rows_in, 2)

    all_blocks = range(blocks)
    inv_a = inverses([kern_ref[b, :width, :width] for b in all_blocks], [inv_a0, inv_a1], nugget, 5, False)
    x_t = [three_pass(kern_ref[b, width:, :width], inv_a[b]) for b in all_blocks]
    missed = [kern_ref[b, width:, :width] - three_pass(x_t[b], kern_ref[b, :width, :width]) for b in all_blocks]
    x_t = [x_t[b] + three_pass(missed[b], inv_a[b]) for b in all_blocks]
    x_n = [x.T for x in x_t]
    schur = [kern_ref[b, width:, width:] - three_pass(x_t[b], kern_ref[b, :width, width:]) for b in all_blocks]
    if len(rounds) > 2:
        hear(1)
        tell(2)
    inv_s = inverses(schur, [inv_s0, inv_s1], nugget, 4, True)

    rim_copy.wait_recv()
    from_peers(rows_in, 2).wait_recv()
    pad = table - points - RIM - n_reg * slots
    value_table = jnp.concatenate(
        [values_ref[...], rim_in[...], rows_in[...].reshape(n_reg * slots, reps), jnp.zeros((pad, reps), F32)],
        axis=0,
    )
    value_parts = split(value_table, 2)
    near_rows = [sum(nn(chosen_ref[b], part) for part in reversed(value_parts)) for b in all_blocks]
    own_rows = [values_ref[b * length : (b + 1) * length, :] for b in all_blocks]
    resids = [own_rows[b] - three_pass(x_t[b], near_rows[b]) for b in all_blocks]
    heads = [three_pass(inv_a[b], near_rows[b]) for b in all_blocks]
    missed = [near_rows[b] - three_pass(kern_ref[b, :width, :width], heads[b]) for b in all_blocks]
    heads = [heads[b] + three_pass(inv_a[b], missed[b]) for b in all_blocks]
    us = [three_pass(inv_s[b], resids[b]) for b in all_blocks]
    backs = [three_pass(x_n[b], us[b]) for b in all_blocks]

    sums = [jnp.zeros((1, 1), F32)] * 3
    for b in all_blocks:
        u, head_back = us[b], -backs[b]
        back = jnp.concatenate([head_back, u], axis=0)
        left = jnp.concatenate([heads[b] + 0.5 * head_back, 0.5 * u], axis=0)
        v = jnp.concatenate(
            [-x_n[b], (iota((length, length), 0) == iota((length, length), 1)).astype(F32)], axis=0
        )
        vs = (-0.5 * reps) * jnp.concatenate([-three_pass(x_n[b], inv_s[b]), inv_s[b]], axis=0)
        left = jnp.concatenate([left, vs], axis=1)
        right = jnp.concatenate([back, v], axis=1)
        grad_kernel = three_pass(left, right, nt)
        total = lambda z: jnp.sum(jnp.sum(z, axis=0, keepdims=True), axis=1, keepdims=True)
        sums = [
            sums[0] + total(grad_kernel * shape_ref[b]),
            sums[1] + total(grad_kernel * slope_ref[b]),
            sums[2] + nugget * total(left * right),
        ]
    lane = iota((1, half), 1)
    mine = jnp.where(lane == 0, sums[0], jnp.where(lane == 1, sums[1], jnp.where(lane == 2, sums[2], 0.0)))
    th_out[...] = mine
    to_peers(lambda peer: th_out, th_in, 5)
    th_in[pl.ds(reg, 1)] = mine[None]

    spread = sum(picked(nn, spread_ref[b], backs[b], 2) for b in all_blocks)
    back_out[...] = spread[points + RIM : points + RIM + n_reg * slots].reshape(n_reg, slots, reps)
    rimback_out[...] = spread[points : points + RIM]
    grad_ref[...] = spread[:points] - jnp.concatenate(us, axis=0)
    if rounds:
        hear(len(rounds) - 1)
    from_peers(th_in, 5).wait_recv()
    band_sum = jnp.sum(th_in[...], axis=0)
    tb_out[...] = band_sum

    def send_band(i, c):
        pltpu.make_async_remote_copy(
            src_ref=tb_out, dst_ref=tb_in.at[band], send_sem=send_sems.at[6], recv_sem=recv_sems.at[6],
            device_id=(band_peer(i), reg), device_id_type=MESH,
        ).start()
        return c

    lax.fori_loop(0, n_band - 1, lambda k, c: send_band(turned(k, n_band), c), 0)
    tb_in[pl.ds(band, 1)] = band_sum[None]
    to_peers(lambda peer: back_out.at[peer], back_in, 3)
    rimback_copy = up_band(rimback_out, rimback_in, 8, n_band - 1)
    rimback_copy.start()

    rimback_copy.wait_recv()
    from_peers(back_in, 3).wait_recv()
    returned = back_in[...].reshape(n_reg * slots, reps)
    grad_ref[...] += picked(tn, sel_ref[...], returned, 2)
    grad_ref[rim_start:, :] += rimback_in[...]

    from_bands = pltpu.make_async_remote_copy(
        src_ref=tb_in.at[pl.ds(0, n_band - 1)], dst_ref=tb_in.at[pl.ds(0, n_band - 1)],
        send_sem=send_sems.at[6], recv_sem=recv_sems.at[6],
        device_id=(band_peer(1), reg), device_id_type=MESH,
    )
    from_bands.wait_recv()
    theta_ref[...] = jnp.sum(tb_in[...], axis=0) * (1.0 / (points * n_band * n_reg * reps))

    from_peers(place_in, 0).wait_send()
    from_peers(ask_in, 1).wait_send()
    from_peers(rows_in, 2).wait_send()
    from_peers(back_in, 3).wait_send()
    from_peers(th_in, 5).wait_send()
    from_bands.wait_send()
    rimplace_copy.wait_send()
    rim_copy.wait_send()
    rimback_copy.wait_send()


def shards(n_band, n_reg, values, coords, neighbours, log_params):
    points, reps = values.shape
    blocks, width = neighbours.shape
    length = points // blocks
    order_n = width + length
    cap = (2 * POOL + n_reg - 2) // (n_reg - 1)
    slots = -(-cap // 16) * 16
    table = -(-(points + RIM + n_reg * slots) // 128) * 128
    half = points // 2
    vmem = lambda *shape: pltpu.VMEM(shape, F32)
    grad, theta = pl.pallas_call(
        functools.partial(kernel, n_band, n_reg, slots),
        out_shape=(pltpu.VMEM((points, reps), F32), pltpu.VMEM((1, half), F32)),
        in_specs=[pl.BlockSpec(memory_space=pltpu.HBM)] * 4,
        out_specs=(pl.BlockSpec(memory_space=pltpu.VMEM), pl.BlockSpec(memory_space=pltpu.VMEM)),
        scratch_shapes=[
            vmem(points, reps), vmem(2, points), pltpu.VMEM((blocks, width), jnp.int32),
            pltpu.SMEM((3,), F32),
            vmem(n_reg, 2, points),
            vmem(n_reg, 2, half), vmem(n_reg, 2, half),
            vmem(n_reg, slots, reps), vmem(n_reg, slots, reps),
            vmem(n_reg, slots, reps), vmem(n_reg, slots, reps),
            vmem(2, half), vmem(RIM, reps), vmem(RIM, reps), vmem(RIM, reps),
            vmem(1, half), vmem(n_reg, 1, half), vmem(1, half), vmem(n_band, 1, half),
            pltpu.VMEM((blocks, width, table), BF16), pltpu.VMEM((blocks, table, width), BF16),
            pltpu.VMEM((n_reg * slots, points), BF16),
            vmem(blocks, order_n, order_n), vmem(blocks, order_n, order_n), vmem(blocks, order_n, order_n),
            vmem(2 * width, width), vmem(2 * width, width), vmem(2 * length, length), vmem(2 * length, length),
            pltpu.SemaphoreType.DMA((4,)), pltpu.SemaphoreType.DMA((9,)), pltpu.SemaphoreType.DMA((9,)),
            pltpu.SemaphoreType.REGULAR((4, 2)),
        ],
        compiler_params=pltpu.CompilerParams(
            collective_id=0, has_side_effects=True, vmem_limit_bytes=60 * 1024 * 1024
        ),
    )(values, coords, neighbours, log_params)
    return grad, theta[0, :3]


def solution(mesh):
    placed = (
        P(("band", "region"), None),
        P(None, ("band", "region")),
        P(("band", "region"), None),
        P(),
    )
    return jax.shard_map(
        functools.partial(shards, mesh.shape["band"], mesh.shape["region"]),
        mesh=mesh,
        in_specs=placed,
        out_specs=(P(("band", "region"), None), P()),
        check_vma=False,
    )
```

```python
import functools

import jax
import jax.numpy as jnp
from jax import lax
from jax.experimental import pallas as pl
from jax.experimental.pallas import tpu as pltpu
from jax.sharding import PartitionSpec as P

MESH = pl.DeviceIdType.MESH
F32 = jnp.float32
BF16 = jnp.bfloat16
M = 256
RIM = 64
POOL = 160


def split(x, parts):
    out = []
    for _ in range(parts - 1):
        high = x.astype(BF16)
        out.append(high)
        x = x - high.astype(F32)
    out.append(x.astype(BF16))
    return out


def nn(a, b):
    return lax.dot_general(a, b, (((1,), (0,)), ((), ())), preferred_element_type=F32)


def nt(a, b):
    return lax.dot_general(a, b, (((1,), (1,)), ((), ())), preferred_element_type=F32)


def tn(a, b):
    return lax.dot_general(a, b, (((0,), (0,)), ((), ())), preferred_element_type=F32)


def three_pass(a, b, dot=nn):
    a_high, a_low = split(a, 2)
    b_high, b_low = split(b, 2)
    n = b.shape[1]
    if dot is nn and n <= 128:
        wide = jnp.concatenate([b_high, b_low], axis=1)
        if a.shape[1] <= 128:
            both = nn(jnp.concatenate([a_high, a_low], axis=1), jnp.concatenate([wide, wide], axis=0))
            return both[:, :n] + both[:, n:]
        both = nn(a_high, wide)
        return both[:, :n] + (both[:, n:] + nn(a_low, b_high))
    return dot(a_high, b_high) + (dot(a_high, b_low) + dot(a_low, b_high))


def picked(dot, chosen, x):
    n = x.shape[1]
    both = dot(chosen, jnp.concatenate(split(x, 2), axis=1))
    return both[:, :n] + both[:, n:]


def iota(shape, dim):
    return lax.broadcasted_iota(jnp.int32, shape, dim)


def inverses(mats, refs, lowest, carried, last):
    n = mats[0].shape[0]
    eye = (iota((n, n), 0) == iota((n, n), 1)).astype(F32)

    def factor_of(product, low):
        scale = 2.0 / (1.0 + low)
        return (2.0 * scale) * eye - (scale * scale) * product

    def raised(low):
        return 4.0 * low / ((1.0 + low) * (1.0 + low))

    lows, overs, factors, starts = [], [], [], []
    for mat in mats:
        sums = jnp.sum(jnp.abs(mat), axis=0, keepdims=True)
        over = 1.0 / (jnp.max(sums, axis=1, keepdims=True) * 1.0001)
        low = lowest * over
        start = over * mat
        factor = factor_of(start, low)
        starts.append(start)
        overs.append(over)
        factors.append(factor)
        lows.append(raised(low))
    products = [three_pass(start, factor) for start, factor in zip(starts, factors)]
    found = [over * factor for over, factor in zip(overs, factors)]
    for _ in range(carried):
        factors = [factor_of(product, low) for product, low in zip(products, lows)]
        found = [three_pass(x, factor) for x, factor in zip(found, factors)]
        products = [three_pass(product, factor) for product, factor in zip(products, factors)]
        lows = [raised(low) for low in lows]
    products = [three_pass(mat, x) for mat, x in zip(mats, found)]
    found = [three_pass(x, factor_of(product, low)) for x, product, low in zip(found, products, lows)]
    if not last:
        return found
    lows = [raised(low) for low in lows]
    products = [three_pass(mat, x) for mat, x in zip(mats, found)]
    return [
        x + three_pass(x, factor_of(product, low) - eye) for x, product, low in zip(found, products, lows)
    ]


def kernel(
    n_band, n_reg, slots,
    values_hbm, coords_hbm, near_hbm, params_hbm,
    grad_ref, theta_ref,
    values_ref, coords_ref, near_ref, params_ref,
    place_in, ask_out, ask_in, rows_out, rows_in, back_out, back_in,
    rimplace_in, rim_in, rimback_out, rimback_in,
    th_out, th_in, tb_out, tb_in,
    chosen_ref, spread_ref, sel_ref, kern_ref, shape_ref, slope_ref, inv_a0, inv_a1, inv_s0, inv_s1,
    local_sems, send_sems, recv_sems, known_sems,
):
    band, reg = lax.axis_index("band"), lax.axis_index("region")
    points, reps = values_ref.shape
    blocks, width = near_ref.shape
    length = points // blocks
    half = points // 2
    order_n = width + length
    rim_start = points - RIM

    def turned(k, n):
        by = (k + 1) // 2
        return lax.rem(n // 2 + jnp.where(lax.rem(k, 2) == 0, by, n - by), n)

    side = 1
    while 2 * (2 * side) ** 2 <= n_reg:
        side *= 2
    tall = n_reg // (2 * side)

    def region_peer(i):
        k = i - 1
        y, x, core = reg // (2 * side), lax.rem(reg // 2, side), lax.rem(reg, 2)
        y = lax.rem(y + turned(k // (2 * side), tall), tall)
        x = lax.rem(x + turned(lax.rem(k // 2, side), side), side)
        core = lax.rem(core + 1 + lax.rem(k, 2), 2)
        return (y * side + x) * 2 + core

    def band_peer(i):
        return lax.rem(band + i, n_band)

    arrivals = [
        pltpu.make_async_copy(source, target, local_sems.at[k])
        for k, (source, target) in enumerate(
            [(coords_hbm, coords_ref), (near_hbm, near_ref), (values_hbm, values_ref), (params_hbm, params_ref)]
        )
    ]
    for copy in arrivals:
        copy.start()

    barrier = pltpu.get_barrier_semaphore()

    def greet_region(i, c):
        pl.semaphore_signal(barrier, inc=1, device_id=(band, region_peer(i)), device_id_type=MESH)
        return c

    for i in (1, n_band - 1):
        pl.semaphore_signal(barrier, inc=1, device_id=(band_peer(i), reg), device_id_type=MESH)
    lax.fori_loop(1, n_reg, greet_region, 0)

    rounds = []
    while 2 ** (len(rounds) + 1) <= n_band // 2:
        rounds.append(2 ** len(rounds))

    def tell(k):
        for side, by in enumerate((rounds[k], n_band - rounds[k])):
            pl.semaphore_signal(
                known_sems.at[k, side], inc=1, device_id=(band_peer(by), reg), device_id_type=MESH
            )

    def hear(k):
        for side in range(2):
            pl.semaphore_wait(known_sems.at[k, side], 1)

    def to_peers(source, into, stage):
        def send(i, c):
            peer = region_peer(i)
            pltpu.make_async_remote_copy(
                src_ref=source(peer), dst_ref=into.at[reg],
                send_sem=send_sems.at[stage], recv_sem=recv_sems.at[stage],
                device_id=(band, peer), device_id_type=MESH,
            ).start()
            return c
        lax.fori_loop(1, n_reg, send, 0)

    def from_peers(into, stage):
        some = pl.ds(0, n_reg - 1)
        return pltpu.make_async_remote_copy(
            src_ref=into.at[some], dst_ref=into.at[some],
            send_sem=send_sems.at[stage], recv_sem=recv_sems.at[stage],
            device_id=(band, region_peer(1)), device_id_type=MESH,
        )

    def up_band(source, into, stage, by):
        return pltpu.make_async_remote_copy(
            src_ref=source, dst_ref=into, send_sem=send_sems.at[stage], recv_sem=recv_sems.at[stage],
            device_id=(band_peer(by), reg), device_id_type=MESH,
        )

    arrivals[0].wait()
    pl.semaphore_wait(barrier, n_reg + 1)
    rimplace_copy = up_band(coords_ref.at[:, pl.ds(half, half)], rimplace_in, 7, 1)
    rimplace_copy.start()
    to_peers(lambda peer: coords_ref, place_in, 0)
    if rounds:
        tell(0)
    place_in[pl.ds(reg, 1)] = coords_ref[...][None]

    arrivals[1].wait()
    near = near_ref[...]
    owner = near // points
    offset = near - owner * points
    owner_band = owner // n_reg
    owner_reg = owner - owner_band * n_reg
    is_rim = owner_band == band - 1
    is_own = jnp.logical_and(owner_band == band, owner_reg == reg)
    is_far = jnp.logical_and(owner_band == band, owner_reg != reg)
    far_row = jnp.where(is_far, owner_reg, -1)
    table_row = jnp.where(is_rim, n_reg, owner_reg)
    off_t = [(iota((points, width), 0) == offset[b : b + 1]).astype(BF16) for b in range(blocks)]
    far_t = [(iota((n_reg, width), 0) == far_row[b : b + 1]).astype(F32) for b in range(blocks)]
    counts = sum(nt(far_t[b].astype(BF16), off_t[b]) for b in range(blocks))
    mask = (counts > 0.5).astype(F32)
    below = (iota((points, points), 0) < iota((points, points), 1)).astype(BF16)
    rank = nn(mask.astype(BF16), below)
    ask_out[:, 0, :] = mask[:, :half]
    ask_out[:, 1, :] = mask[:, half:]
    to_peers(lambda peer: ask_out.at[peer], ask_in, 1)
    arrivals[2].wait()
    rim_copy = up_band(values_ref.at[pl.ds(rim_start, RIM)], rim_in, 4, 1)
    rim_copy.start()
    ask_in[pl.ds(reg, 1)] = jnp.zeros((1, 2, half), F32)
    rows_in[pl.ds(reg, 1)] = jnp.zeros((1, slots, reps), F32)
    back_in[pl.ds(reg, 1)] = jnp.zeros((1, slots, reps), F32)

    rank_bf = rank.astype(BF16)
    index_rows = []
    for b in range(blocks):
        slot = jnp.sum(far_t[b] * nn(rank_bf, off_t[b]), axis=0, keepdims=True).astype(jnp.int32)
        far_index = points + RIM + owner_reg[b : b + 1] * slots + slot
        rim_index = points + offset[b : b + 1] - rim_start
        index_rows.append(
            jnp.where(is_own[b : b + 1], offset[b : b + 1], jnp.where(is_rim[b : b + 1], rim_index, far_index))
        )
    table = chosen_ref.shape[2]
    index_cols = jnp.concatenate(index_rows + [jnp.zeros((8 - blocks, width), jnp.int32)], axis=0).astype(F32).T
    for b in range(blocks):
        column = index_cols[:, b : b + 1].astype(jnp.int32)
        chosen_ref[b] = (iota((width, table), 1) == column).astype(BF16)
        spread_ref[b] = (iota((table, width), 0) == index_rows[b]).astype(BF16)

    arrivals[3].wait()
    from_peers(place_in, 0).wait_recv()
    rimplace_copy.wait_recv()

    x_row, y_row = coords_ref[0:1, :], coords_ref[1:2, :]
    zero_half = jnp.zeros((1, half), F32)
    tables = []
    for k in range(2):
        rim_row = jnp.concatenate([zero_half, rimplace_in[k : k + 1, :]], axis=1)
        tables += [place_in[:, k, :], rim_row, jnp.zeros((7, points), F32)]
    coord_table = jnp.concatenate(tables, axis=0)
    rows = n_reg + 8
    variance = jnp.exp(jnp.full((1, 1), params_ref[0], F32))
    inverse_range = jnp.sqrt(jnp.full((1, 1), 3.0, F32)) * jnp.exp(jnp.full((1, 1), -params_ref[1], F32))
    nugget = jnp.exp(jnp.full((1, 1), params_ref[2], F32))
    parts = split(coord_table, 3)
    for b in range(blocks):
        own_t = (iota((rows, width), 0) == table_row[b : b + 1]).astype(F32)
        found = sum(nn(part, off_t[b]) for part in reversed(parts))
        x_near = jnp.sum(own_t * found[:rows], axis=0, keepdims=True)
        y_near = jnp.sum(own_t * found[rows:], axis=0, keepdims=True)
        here = slice(b * length, (b + 1) * length)
        x_joint = jnp.concatenate([x_near, x_row[:, here]], axis=1)
        y_joint = jnp.concatenate([y_near, y_row[:, here]], axis=1)
        cols = jnp.concatenate([x_joint, y_joint, jnp.zeros((6, order_n), F32)], axis=0).T
        delta_x = cols[:, 0:1] - x_joint
        delta_y = cols[:, 1:2] - y_joint
        scaled = inverse_range * jnp.sqrt(delta_x * delta_x + delta_y * delta_y)
        decayed = variance * jnp.exp(-scaled)
        shape_part = decayed + scaled * decayed
        shape_ref[b] = shape_part
        slope_ref[b] = scaled * scaled * decayed
        diagonal = iota((order_n, order_n), 0) == iota((order_n, order_n), 1)
        kern_ref[b] = jnp.where(diagonal, shape_part + nugget, shape_part)

    from_peers(ask_in, 1).wait_recv()
    wanted = jnp.concatenate([ask_in[:, 0, :], ask_in[:, 1, :]], axis=1)
    wanted_rank = nn(wanted.astype(BF16), below)
    slot_of = jnp.where(wanted > 0.5, wanted_rank, -1.0)
    sel = (
        jnp.broadcast_to(slot_of[:, None, :], (n_reg, slots, points))
        == iota((n_reg, slots, points), 1).astype(F32)
    )
    sel_ref[...] = sel.astype(F32).reshape(n_reg * slots, points).astype(BF16)
    rows_out[...] = picked(nn, sel_ref[...], values_ref[...]).reshape(n_reg, slots, reps)
    to_peers(lambda peer: rows_out.at[peer], rows_in, 2)

    all_blocks = range(blocks)
    inv_a = inverses([kern_ref[b, :width, :width] for b in all_blocks], [inv_a0, inv_a1], nugget, 5, False)
    x_t = [three_pass(kern_ref[b, width:, :width], inv_a[b]) for b in all_blocks]
    missed = [kern_ref[b, width:, :width] - three_pass(x_t[b], kern_ref[b, :width, :width]) for b in all_blocks]
    x_t = [x_t[b] + three_pass(missed[b], inv_a[b]) for b in all_blocks]
    x_n = [x.T for x in x_t]
    schur = [kern_ref[b, width:, width:] - three_pass(x_t[b], kern_ref[b, :width, width:]) for b in all_blocks]
    if len(rounds) > 1:
        hear(0)
        tell(1)
    inv_s = inverses(schur, [inv_s0, inv_s1], nugget, 4, True)

    if len(rounds) > 2:
        hear(1)
        tell(2)
    rim_copy.wait_recv()
    from_peers(rows_in, 2).wait_recv()
    pad = table - points - RIM - n_reg * slots
    value_table = jnp.concatenate(
        [values_ref[...], rim_in[...], rows_in[...].reshape(n_reg * slots, reps), jnp.zeros((pad, reps), F32)],
        axis=0,
    )
    near_rows = [picked(nn, chosen_ref[b], value_table) for b in all_blocks]
    own_rows = [values_ref[b * length : (b + 1) * length, :] for b in all_blocks]
    resids = [own_rows[b] - three_pass(x_t[b], near_rows[b]) for b in all_blocks]
    heads = [three_pass(inv_a[b], near_rows[b]) for b in all_blocks]
    missed = [near_rows[b] - three_pass(kern_ref[b, :width, :width], heads[b]) for b in all_blocks]
    heads = [heads[b] + three_pass(inv_a[b], missed[b]) for b in all_blocks]
    us = [three_pass(inv_s[b], resids[b]) for b in all_blocks]
    backs = [three_pass(x_n[b], us[b]) for b in all_blocks]

    sums = [jnp.zeros((1, 1), F32)] * 3
    for b in all_blocks:
        u, head_back = us[b], -backs[b]
        back = jnp.concatenate([head_back, u], axis=0)
        left = jnp.concatenate([heads[b] + 0.5 * head_back, 0.5 * u], axis=0)
        v = jnp.concatenate(
            [-x_n[b], (iota((length, length), 0) == iota((length, length), 1)).astype(F32)], axis=0
        )
        vs = (-0.5 * reps) * jnp.concatenate([-three_pass(x_n[b], inv_s[b]), inv_s[b]], axis=0)
        left = jnp.concatenate([left, vs], axis=1)
        right = jnp.concatenate([back, v], axis=1)
        grad_kernel = three_pass(left, right, nt)
        total = lambda z: jnp.sum(jnp.sum(z, axis=0, keepdims=True), axis=1, keepdims=True)
        sums = [
            sums[0] + total(grad_kernel * shape_ref[b]),
            sums[1] + total(grad_kernel * slope_ref[b]),
            sums[2] + nugget * total(left * right),
        ]
    lane = iota((1, half), 1)
    mine = jnp.where(lane == 0, sums[0], jnp.where(lane == 1, sums[1], jnp.where(lane == 2, sums[2], 0.0)))
    th_out[...] = mine
    to_peers(lambda peer: th_out, th_in, 5)
    th_in[pl.ds(reg, 1)] = mine[None]

    spread = sum(picked(nn, spread_ref[b], backs[b]) for b in all_blocks)
    back_out[...] = spread[points + RIM : points + RIM + n_reg * slots].reshape(n_reg, slots, reps)
    rimback_out[...] = spread[points : points + RIM]
    grad_ref[...] = spread[:points] - jnp.concatenate(us, axis=0)
    if rounds:
        hear(len(rounds) - 1)
    from_peers(th_in, 5).wait_recv()
    band_sum = jnp.sum(th_in[...], axis=0)
    tb_out[...] = band_sum

    def send_band(i, c):
        pltpu.make_async_remote_copy(
            src_ref=tb_out, dst_ref=tb_in.at[band], send_sem=send_sems.at[6], recv_sem=recv_sems.at[6],
            device_id=(band_peer(i), reg), device_id_type=MESH,
        ).start()
        return c

    lax.fori_loop(0, n_band - 1, lambda k, c: send_band(turned(k, n_band), c), 0)
    tb_in[pl.ds(band, 1)] = band_sum[None]
    to_peers(lambda peer: back_out.at[peer], back_in, 3)
    rimback_copy = up_band(rimback_out, rimback_in, 8, n_band - 1)
    rimback_copy.start()

    rimback_copy.wait_recv()
    from_peers(back_in, 3).wait_recv()
    returned = back_in[...].reshape(n_reg * slots, reps)
    grad_ref[...] += picked(tn, sel_ref[...], returned)
    grad_ref[rim_start:, :] += rimback_in[...]

    from_bands = pltpu.make_async_remote_copy(
        src_ref=tb_in.at[pl.ds(0, n_band - 1)], dst_ref=tb_in.at[pl.ds(0, n_band - 1)],
        send_sem=send_sems.at[6], recv_sem=recv_sems.at[6],
        device_id=(band_peer(1), reg), device_id_type=MESH,
    )
    from_bands.wait_recv()
    theta_ref[...] = jnp.sum(tb_in[...], axis=0) * (1.0 / (points * n_band * n_reg * reps))

    from_peers(place_in, 0).wait_send()
    from_peers(ask_in, 1).wait_send()
    from_peers(rows_in, 2).wait_send()
    from_peers(back_in, 3).wait_send()
    from_peers(th_in, 5).wait_send()
    from_bands.wait_send()
    rimplace_copy.wait_send()
    rim_copy.wait_send()
    rimback_copy.wait_send()


def shards(n_band, n_reg, values, coords, neighbours, log_params):
    points, reps = values.shape
    blocks, width = neighbours.shape
    length = points // blocks
    order_n = width + length
    cap = (2 * POOL + n_reg - 2) // (n_reg - 1)
    slots = -(-cap // 16) * 16
    table = -(-(points + RIM + n_reg * slots) // 128) * 128
    half = points // 2
    vmem = lambda *shape: pltpu.VMEM(shape, F32)
    grad, theta = pl.pallas_call(
        functools.partial(kernel, n_band, n_reg, slots),
        out_shape=(pltpu.VMEM((points, reps), F32), pltpu.VMEM((1, half), F32)),
        in_specs=[pl.BlockSpec(memory_space=pltpu.HBM)] * 4,
        out_specs=(pl.BlockSpec(memory_space=pltpu.VMEM), pl.BlockSpec(memory_space=pltpu.VMEM)),
        scratch_shapes=[
            vmem(points, reps), vmem(2, points), pltpu.VMEM((blocks, width), jnp.int32),
            pltpu.SMEM((3,), F32),
            vmem(n_reg, 2, points),
            vmem(n_reg, 2, half), vmem(n_reg, 2, half),
            vmem(n_reg, slots, reps), vmem(n_reg, slots, reps),
            vmem(n_reg, slots, reps), vmem(n_reg, slots, reps),
            vmem(2, half), vmem(RIM, reps), vmem(RIM, reps), vmem(RIM, reps),
            vmem(1, half), vmem(n_reg, 1, half), vmem(1, half), vmem(n_band, 1, half),
            pltpu.VMEM((blocks, width, table), BF16), pltpu.VMEM((blocks, table, width), BF16),
            pltpu.VMEM((n_reg * slots, points), BF16),
            vmem(blocks, order_n, order_n), vmem(blocks, order_n, order_n), vmem(blocks, order_n, order_n),
            vmem(2 * width, width), vmem(2 * width, width), vmem(2 * length, length), vmem(2 * length, length),
            pltpu.SemaphoreType.DMA((4,)), pltpu.SemaphoreType.DMA((9,)), pltpu.SemaphoreType.DMA((9,)),
            pltpu.SemaphoreType.REGULAR((4, 2)),
        ],
        compiler_params=pltpu.CompilerParams(
            collective_id=0, has_side_effects=True, vmem_limit_bytes=60 * 1024 * 1024
        ),
    )(values, coords, neighbours, log_params)
    return grad, theta[0, :3]


def solution(mesh):
    placed = (
        P(("band", "region"), None),
        P(None, ("band", "region")),
        P(("band", "region"), None),
        P(),
    )
    return jax.shard_map(
        functools.partial(shards, mesh.shape["band"], mesh.shape["region"]),
        mesh=mesh,
        in_specs=placed,
        out_specs=(P(("band", "region"), None), P()),
        check_vma=False,
    )
```

```python
import functools

import jax
import jax.numpy as jnp
from jax import lax
from jax.experimental import pallas as pl
from jax.experimental.pallas import tpu as pltpu
from jax.sharding import PartitionSpec as P

MESH = pl.DeviceIdType.MESH
F32 = jnp.float32
BF16 = jnp.bfloat16
M = 256
RIM = 64
POOL = 160


def split(x, parts):
    out = []
    for _ in range(parts - 1):
        high = x.astype(BF16)
        out.append(high)
        x = x - high.astype(F32)
    out.append(x.astype(BF16))
    return out


def nn(a, b):
    return lax.dot_general(a, b, (((1,), (0,)), ((), ())), preferred_element_type=F32)


def nt(a, b):
    return lax.dot_general(a, b, (((1,), (1,)), ((), ())), preferred_element_type=F32)


def tn(a, b):
    return lax.dot_general(a, b, (((0,), (0,)), ((), ())), preferred_element_type=F32)


def three_pass(a, b, dot=nn):
    a_high, a_low = split(a, 2)
    b_high, b_low = split(b, 2)
    n = b.shape[1]
    if dot is nn and n <= 128:
        wide = jnp.concatenate([b_high, b_low], axis=1)
        if a.shape[1] <= 128:
            both = nn(jnp.concatenate([a_high, a_low], axis=1), jnp.concatenate([wide, wide], axis=0))
            return both[:, :n] + both[:, n:]
        both = nn(a_high, wide)
        return both[:, :n] + (both[:, n:] + nn(a_low, b_high))
    return dot(a_high, b_high) + (dot(a_high, b_low) + dot(a_low, b_high))


def picked(dot, chosen, x):
    n = x.shape[1]
    both = dot(chosen, jnp.concatenate(split(x, 2), axis=1))
    return both[:, :n] + both[:, n:]


def iota(shape, dim):
    return lax.broadcasted_iota(jnp.int32, shape, dim)


def inverses(mats, lowest, carried, last):
    n = mats[0].shape[0]
    eye = (iota((n, n), 0) == iota((n, n), 1)).astype(F32)

    def factor_of(product, low):
        scale = 2.0 / (1.0 + low)
        return (2.0 * scale) * eye - (scale * scale) * product

    def raised(low):
        return 4.0 * low / ((1.0 + low) * (1.0 + low))

    lows, overs, factors, starts = [], [], [], []
    for mat in mats:
        sums = jnp.sum(jnp.abs(mat), axis=0, keepdims=True)
        over = 1.0 / (jnp.max(sums, axis=1, keepdims=True) * 1.0001)
        low = lowest * over
        start = over * mat
        factor = factor_of(start, low)
        starts.append(start)
        overs.append(over)
        factors.append(factor)
        lows.append(raised(low))
    products = [three_pass(start, factor) for start, factor in zip(starts, factors)]
    found = [over * factor for over, factor in zip(overs, factors)]
    for _ in range(carried):
        factors = [factor_of(product, low) for product, low in zip(products, lows)]
        found = [three_pass(x, factor) for x, factor in zip(found, factors)]
        products = [three_pass(product, factor) for product, factor in zip(products, factors)]
        lows = [raised(low) for low in lows]
    products = [three_pass(mat, x) for mat, x in zip(mats, found)]
    found = [three_pass(x, factor_of(product, low)) for x, product, low in zip(found, products, lows)]
    if not last:
        return found
    lows = [raised(low) for low in lows]
    products = [three_pass(mat, x) for mat, x in zip(mats, found)]
    return [
        x + three_pass(x, factor_of(product, low) - eye) for x, product, low in zip(found, products, lows)
    ]


def kernel(
    n_band, n_reg, slots,
    values_hbm, coords_hbm, near_hbm, params_hbm,
    grad_ref, theta_ref,
    values_ref, coords_ref, near_ref, params_ref,
    place_in, ask_out, ask_in, rows_out, rows_in, back_out, back_in,
    rimplace_in, rim_in, rimback_out, rimback_in,
    th_out, th_in, tb_out, tb_in,
    chosen_ref, spread_ref, sel_ref, kern_ref, shape_ref, slope_ref,
    local_sems, send_sems, recv_sems, known_sems,
):
    band, reg = lax.axis_index("band"), lax.axis_index("region")
    points, reps = values_ref.shape
    blocks, width = near_ref.shape
    length = points // blocks
    half = points // 2
    order_n = width + length
    rim_start = points - RIM

    def turned(k, n):
        by = (k + 1) // 2
        return lax.rem(n // 2 + jnp.where(lax.rem(k, 2) == 0, by, n - by), n)

    side = 1
    while 2 * (2 * side) ** 2 <= n_reg:
        side *= 2
    tall = n_reg // (2 * side)

    def region_peer(i):
        k = i - 1
        y, x, core = reg // (2 * side), lax.rem(reg // 2, side), lax.rem(reg, 2)
        y = lax.rem(y + turned(k // (2 * side), tall), tall)
        x = lax.rem(x + turned(lax.rem(k // 2, side), side), side)
        core = lax.rem(core + 1 + lax.rem(k, 2), 2)
        return (y * side + x) * 2 + core

    def band_peer(i):
        return lax.rem(band + i, n_band)

    arrivals = [
        pltpu.make_async_copy(source, target, local_sems.at[k])
        for k, (source, target) in enumerate(
            [(coords_hbm, coords_ref), (near_hbm, near_ref), (values_hbm, values_ref), (params_hbm, params_ref)]
        )
    ]
    for copy in arrivals:
        copy.start()

    barrier = pltpu.get_barrier_semaphore()

    def greet_region(i, c):
        pl.semaphore_signal(barrier, inc=1, device_id=(band, region_peer(i)), device_id_type=MESH)
        return c

    for i in (1, n_band - 1):
        pl.semaphore_signal(barrier, inc=1, device_id=(band_peer(i), reg), device_id_type=MESH)
    lax.fori_loop(1, n_reg, greet_region, 0)

    rounds = []
    while 2 ** (len(rounds) + 1) <= n_band // 2:
        rounds.append(2 ** len(rounds))

    def tell(k):
        for side, by in enumerate((rounds[k], n_band - rounds[k])):
            pl.semaphore_signal(
                known_sems.at[k, side], inc=1, device_id=(band_peer(by), reg), device_id_type=MESH
            )

    def hear(k):
        for side in range(2):
            pl.semaphore_wait(known_sems.at[k, side], 1)

    def to_peers(source, into, stage):
        def send(i, c):
            peer = region_peer(i)
            pltpu.make_async_remote_copy(
                src_ref=source(peer), dst_ref=into.at[reg],
                send_sem=send_sems.at[stage], recv_sem=recv_sems.at[stage],
                device_id=(band, peer), device_id_type=MESH,
            ).start()
            return c
        lax.fori_loop(1, n_reg, send, 0)

    def from_peers(into, stage):
        some = pl.ds(0, n_reg - 1)
        return pltpu.make_async_remote_copy(
            src_ref=into.at[some], dst_ref=into.at[some],
            send_sem=send_sems.at[stage], recv_sem=recv_sems.at[stage],
            device_id=(band, region_peer(1)), device_id_type=MESH,
        )

    def up_band(source, into, stage, by):
        return pltpu.make_async_remote_copy(
            src_ref=source, dst_ref=into, send_sem=send_sems.at[stage], recv_sem=recv_sems.at[stage],
            device_id=(band_peer(by), reg), device_id_type=MESH,
        )

    arrivals[0].wait()
    pl.semaphore_wait(barrier, n_reg + 1)
    rimplace_copy = up_band(coords_ref.at[:, pl.ds(half, half)], rimplace_in, 7, 1)
    rimplace_copy.start()
    to_peers(lambda peer: coords_ref, place_in, 0)
    if rounds:
        tell(0)
    place_in[pl.ds(reg, 1)] = coords_ref[...][None]

    arrivals[1].wait()
    near = near_ref[...]
    owner = near // points
    offset = near - owner * points
    owner_band = owner // n_reg
    owner_reg = owner - owner_band * n_reg
    is_rim = owner_band == band - 1
    is_own = jnp.logical_and(owner_band == band, owner_reg == reg)
    is_far = jnp.logical_and(owner_band == band, owner_reg != reg)
    far_row = jnp.where(is_far, owner_reg, -1)
    table_row = jnp.where(is_rim, n_reg, owner_reg)
    off_t = [(iota((points, width), 0) == offset[b : b + 1]).astype(BF16) for b in range(blocks)]
    far_t = [(iota((n_reg, width), 0) == far_row[b : b + 1]).astype(F32) for b in range(blocks)]
    counts = sum(nt(far_t[b].astype(BF16), off_t[b]) for b in range(blocks))
    mask = (counts > 0.5).astype(F32)
    below = (iota((points, points), 0) < iota((points, points), 1)).astype(BF16)
    rank = nn(mask.astype(BF16), below)
    ask_out[:, 0, :] = mask[:, :half]
    ask_out[:, 1, :] = mask[:, half:]
    to_peers(lambda peer: ask_out.at[peer], ask_in, 1)
    arrivals[2].wait()
    rim_copy = up_band(values_ref.at[pl.ds(rim_start, RIM)], rim_in, 4, 1)
    rim_copy.start()
    ask_in[pl.ds(reg, 1)] = jnp.zeros((1, 2, half), F32)
    rows_in[pl.ds(reg, 1)] = jnp.zeros((1, slots, reps), F32)
    back_in[pl.ds(reg, 1)] = jnp.zeros((1, slots, reps), F32)

    rank_bf = rank.astype(BF16)
    index_rows = []
    for b in range(blocks):
        slot = jnp.sum(far_t[b] * nn(rank_bf, off_t[b]), axis=0, keepdims=True).astype(jnp.int32)
        far_index = points + RIM + owner_reg[b : b + 1] * slots + slot
        rim_index = points + offset[b : b + 1] - rim_start
        index_rows.append(
            jnp.where(is_own[b : b + 1], offset[b : b + 1], jnp.where(is_rim[b : b + 1], rim_index, far_index))
        )
    table = chosen_ref.shape[2]
    index_cols = jnp.concatenate(index_rows + [jnp.zeros((8 - blocks, width), jnp.int32)], axis=0).astype(F32).T
    for b in range(blocks):
        column = index_cols[:, b : b + 1].astype(jnp.int32)
        chosen_ref[b] = (iota((width, table), 1) == column).astype(BF16)
        spread_ref[b] = (iota((table, width), 0) == index_rows[b]).astype(BF16)

    arrivals[3].wait()
    from_peers(place_in, 0).wait_recv()
    rimplace_copy.wait_recv()

    x_row, y_row = coords_ref[0:1, :], coords_ref[1:2, :]
    zero_half = jnp.zeros((1, half), F32)
    tables = []
    for k in range(2):
        rim_row = jnp.concatenate([zero_half, rimplace_in[k : k + 1, :]], axis=1)
        tables += [place_in[:, k, :], rim_row, jnp.zeros((7, points), F32)]
    coord_table = jnp.concatenate(tables, axis=0)
    rows = n_reg + 8
    variance = jnp.exp(jnp.full((1, 1), params_ref[0], F32))
    inverse_range = jnp.sqrt(jnp.full((1, 1), 3.0, F32)) * jnp.exp(jnp.full((1, 1), -params_ref[1], F32))
    nugget = jnp.exp(jnp.full((1, 1), params_ref[2], F32))
    parts = split(coord_table, 3)
    for b in range(blocks):
        own_t = (iota((rows, width), 0) == table_row[b : b + 1]).astype(F32)
        found = sum(nn(part, off_t[b]) for part in reversed(parts))
        x_near = jnp.sum(own_t * found[:rows], axis=0, keepdims=True)
        y_near = jnp.sum(own_t * found[rows:], axis=0, keepdims=True)
        here = slice(b * length, (b + 1) * length)
        x_joint = jnp.concatenate([x_near, x_row[:, here]], axis=1)
        y_joint = jnp.concatenate([y_near, y_row[:, here]], axis=1)
        cols = jnp.concatenate([x_joint, y_joint, jnp.zeros((6, order_n), F32)], axis=0).T
        delta_x = cols[:, 0:1] - x_joint
        delta_y = cols[:, 1:2] - y_joint
        scaled = inverse_range * jnp.sqrt(delta_x * delta_x + delta_y * delta_y)
        decayed = variance * jnp.exp(-scaled)
        shape_part = decayed + scaled * decayed
        shape_ref[b] = shape_part
        slope_ref[b] = scaled * scaled * decayed
        diagonal = iota((order_n, order_n), 0) == iota((order_n, order_n), 1)
        kern_ref[b] = jnp.where(diagonal, shape_part + nugget, shape_part)

    from_peers(ask_in, 1).wait_recv()
    wanted = jnp.concatenate([ask_in[:, 0, :], ask_in[:, 1, :]], axis=1)
    wanted_rank = nn(wanted.astype(BF16), below)
    slot_of = jnp.where(wanted > 0.5, wanted_rank, -1.0)
    sel = (
        jnp.broadcast_to(slot_of[:, None, :], (n_reg, slots, points))
        == iota((n_reg, slots, points), 1).astype(F32)
    )
    sel_ref[...] = sel.astype(F32).reshape(n_reg * slots, points).astype(BF16)
    rows_out[...] = picked(nn, sel_ref[...], values_ref[...]).reshape(n_reg, slots, reps)
    to_peers(lambda peer: rows_out.at[peer], rows_in, 2)

    if len(rounds) > 1:
        hear(0)
        tell(1)
    all_blocks = range(blocks)
    inv_a = inverses([kern_ref[b, :width, :width] for b in all_blocks], nugget, 5, False)
    x_t = [three_pass(kern_ref[b, width:, :width], inv_a[b]) for b in all_blocks]
    missed = [kern_ref[b, width:, :width] - three_pass(x_t[b], kern_ref[b, :width, :width]) for b in all_blocks]
    x_t = [x_t[b] + three_pass(missed[b], inv_a[b]) for b in all_blocks]
    x_n = [x.T for x in x_t]
    schur = [kern_ref[b, width:, width:] - three_pass(x_t[b], kern_ref[b, :width, width:]) for b in all_blocks]
    inv_s = inverses(schur, nugget, 4, True)

    if len(rounds) > 2:
        hear(1)
        tell(2)
    rim_copy.wait_recv()
    from_peers(rows_in, 2).wait_recv()
    pad = table - points - RIM - n_reg * slots
    value_table = jnp.concatenate(
        [values_ref[...], rim_in[...], rows_in[...].reshape(n_reg * slots, reps), jnp.zeros((pad, reps), F32)],
        axis=0,
    )
    near_rows = [picked(nn, chosen_ref[b], value_table) for b in all_blocks]
    own_rows = [values_ref[b * length : (b + 1) * length, :] for b in all_blocks]
    resids = [own_rows[b] - three_pass(x_t[b], near_rows[b]) for b in all_blocks]
    heads = [three_pass(inv_a[b], near_rows[b]) for b in all_blocks]
    missed = [near_rows[b] - three_pass(kern_ref[b, :width, :width], heads[b]) for b in all_blocks]
    heads = [heads[b] + three_pass(inv_a[b], missed[b]) for b in all_blocks]
    us = [three_pass(inv_s[b], resids[b]) for b in all_blocks]
    backs = [three_pass(x_n[b], us[b]) for b in all_blocks]

    sums = [jnp.zeros((1, 1), F32)] * 3
    for b in all_blocks:
        u, head_back = us[b], -backs[b]
        back = jnp.concatenate([head_back, u], axis=0)
        left = jnp.concatenate([heads[b] + 0.5 * head_back, 0.5 * u], axis=0)
        v = jnp.concatenate(
            [-x_n[b], (iota((length, length), 0) == iota((length, length), 1)).astype(F32)], axis=0
        )
        vs = (-0.5 * reps) * jnp.concatenate([-three_pass(x_n[b], inv_s[b]), inv_s[b]], axis=0)
        left = jnp.concatenate([left, vs], axis=1)
        right = jnp.concatenate([back, v], axis=1)
        grad_kernel = three_pass(left, right, nt)
        total = lambda z: jnp.sum(jnp.sum(z, axis=0, keepdims=True), axis=1, keepdims=True)
        sums = [
            sums[0] + total(grad_kernel * shape_ref[b]),
            sums[1] + total(grad_kernel * slope_ref[b]),
            sums[2] + nugget * total(left * right),
        ]
    lane = iota((1, half), 1)
    mine = jnp.where(lane == 0, sums[0], jnp.where(lane == 1, sums[1], jnp.where(lane == 2, sums[2], 0.0)))
    th_out[...] = mine
    to_peers(lambda peer: th_out, th_in, 5)
    th_in[pl.ds(reg, 1)] = mine[None]

    spread = sum(picked(nn, spread_ref[b], backs[b]) for b in all_blocks)
    back_out[...] = spread[points + RIM : points + RIM + n_reg * slots].reshape(n_reg, slots, reps)
    rimback_out[...] = spread[points : points + RIM]
    grad_ref[...] = spread[:points] - jnp.concatenate(us, axis=0)
    if rounds:
        hear(len(rounds) - 1)
    from_peers(th_in, 5).wait_recv()
    band_sum = jnp.sum(th_in[...], axis=0)
    tb_out[...] = band_sum

    def send_band(i, c):
        pltpu.make_async_remote_copy(
            src_ref=tb_out, dst_ref=tb_in.at[band], send_sem=send_sems.at[6], recv_sem=recv_sems.at[6],
            device_id=(band_peer(i), reg), device_id_type=MESH,
        ).start()
        return c

    lax.fori_loop(0, n_band - 1, lambda k, c: send_band(turned(k, n_band), c), 0)
    tb_in[pl.ds(band, 1)] = band_sum[None]
    to_peers(lambda peer: back_out.at[peer], back_in, 3)
    rimback_copy = up_band(rimback_out, rimback_in, 8, n_band - 1)
    rimback_copy.start()

    rimback_copy.wait_recv()
    from_peers(back_in, 3).wait_recv()
    returned = back_in[...].reshape(n_reg * slots, reps)
    grad_ref[...] += picked(tn, sel_ref[...], returned)
    grad_ref[rim_start:, :] += rimback_in[...]

    from_bands = pltpu.make_async_remote_copy(
        src_ref=tb_in.at[pl.ds(0, n_band - 1)], dst_ref=tb_in.at[pl.ds(0, n_band - 1)],
        send_sem=send_sems.at[6], recv_sem=recv_sems.at[6],
        device_id=(band_peer(1), reg), device_id_type=MESH,
    )
    from_bands.wait_recv()
    theta_ref[...] = jnp.sum(tb_in[...], axis=0) * (1.0 / (points * n_band * n_reg * reps))

    from_peers(place_in, 0).wait_send()
    from_peers(ask_in, 1).wait_send()
    from_peers(rows_in, 2).wait_send()
    from_peers(back_in, 3).wait_send()
    from_peers(th_in, 5).wait_send()
    from_bands.wait_send()
    rimplace_copy.wait_send()
    rim_copy.wait_send()
    rimback_copy.wait_send()


def shards(n_band, n_reg, values, coords, neighbours, log_params):
    points, reps = values.shape
    blocks, width = neighbours.shape
    length = points // blocks
    order_n = width + length
    cap = (2 * POOL + n_reg - 2) // (n_reg - 1)
    slots = -(-cap // 16) * 16
    table = -(-(points + RIM + n_reg * slots) // 128) * 128
    half = points // 2
    vmem = lambda *shape: pltpu.VMEM(shape, F32)
    grad, theta = pl.pallas_call(
        functools.partial(kernel, n_band, n_reg, slots),
        out_shape=(pltpu.VMEM((points, reps), F32), pltpu.VMEM((1, half), F32)),
        in_specs=[pl.BlockSpec(memory_space=pltpu.HBM)] * 4,
        out_specs=(pl.BlockSpec(memory_space=pltpu.VMEM), pl.BlockSpec(memory_space=pltpu.VMEM)),
        scratch_shapes=[
            vmem(points, reps), vmem(2, points), pltpu.VMEM((blocks, width), jnp.int32),
            pltpu.SMEM((3,), F32),
            vmem(n_reg, 2, points),
            vmem(n_reg, 2, half), vmem(n_reg, 2, half),
            vmem(n_reg, slots, reps), vmem(n_reg, slots, reps),
            vmem(n_reg, slots, reps), vmem(n_reg, slots, reps),
            vmem(2, half), vmem(RIM, reps), vmem(RIM, reps), vmem(RIM, reps),
            vmem(1, half), vmem(n_reg, 1, half), vmem(1, half), vmem(n_band, 1, half),
            pltpu.VMEM((blocks, width, table), BF16), pltpu.VMEM((blocks, table, width), BF16),
            pltpu.VMEM((n_reg * slots, points), BF16),
            vmem(blocks, order_n, order_n), vmem(blocks, order_n, order_n), vmem(blocks, order_n, order_n),
            pltpu.SemaphoreType.DMA((4,)), pltpu.SemaphoreType.DMA((9,)), pltpu.SemaphoreType.DMA((9,)),
            pltpu.SemaphoreType.REGULAR((4, 2)),
        ],
        compiler_params=pltpu.CompilerParams(
            collective_id=0, has_side_effects=True, vmem_limit_bytes=60 * 1024 * 1024
        ),
    )(values, coords, neighbours, log_params)
    return grad, theta[0, :3]


def solution(mesh):
    placed = (
        P(("band", "region"), None),
        P(None, ("band", "region")),
        P(("band", "region"), None),
        P(),
    )
    return jax.shard_map(
        functools.partial(shards, mesh.shape["band"], mesh.shape["region"]),
        mesh=mesh,
        in_specs=placed,
        out_specs=(P(("band", "region"), None), P()),
        check_vma=False,
    )
```

```python
import functools

import jax
import jax.numpy as jnp
from jax import lax
from jax.experimental import pallas as pl
from jax.experimental.pallas import tpu as pltpu
from jax.sharding import PartitionSpec as P

MESH = pl.DeviceIdType.MESH
F32 = jnp.float32
BF16 = jnp.bfloat16
M = 256
RIM = 64
POOL = 160


def split(x, parts):
    out = []
    for _ in range(parts - 1):
        high = x.astype(BF16)
        out.append(high)
        x = x - high.astype(F32)
    out.append(x.astype(BF16))
    return out


def nn(a, b):
    return lax.dot_general(a, b, (((1,), (0,)), ((), ())), preferred_element_type=F32)


def nt(a, b):
    return lax.dot_general(a, b, (((1,), (1,)), ((), ())), preferred_element_type=F32)


def tn(a, b):
    return lax.dot_general(a, b, (((0,), (0,)), ((), ())), preferred_element_type=F32)


def three_pass(a, b, dot=nn):
    a_high, a_low = split(a, 2)
    b_high, b_low = split(b, 2)
    n = b.shape[1]
    if dot is nn and n <= 128:
        wide = jnp.concatenate([b_high, b_low], axis=1)
        if a.shape[1] <= 128:
            both = nn(jnp.concatenate([a_high, a_low], axis=1), jnp.concatenate([wide, wide], axis=0))
            return both[:, :n] + both[:, n:]
        both = nn(a_high, wide)
        return both[:, :n] + (both[:, n:] + nn(a_low, b_high))
    return dot(a_high, b_high) + (dot(a_high, b_low) + dot(a_low, b_high))


def picked(dot, chosen, x):
    n = x.shape[1]
    both = dot(chosen, jnp.concatenate(split(x, 2), axis=1))
    return both[:, :n] + both[:, n:]


def iota(shape, dim):
    return lax.broadcasted_iota(jnp.int32, shape, dim)


def inverses(mats, lowest, carried, last):
    n = mats[0].shape[0]
    eye = (iota((n, n), 0) == iota((n, n), 1)).astype(F32)

    def factor_of(product, low):
        scale = 2.0 / (1.0 + low)
        return (2.0 * scale) * eye - (scale * scale) * product

    def raised(low):
        return 4.0 * low / ((1.0 + low) * (1.0 + low))

    lows, overs, factors, starts = [], [], [], []
    for mat in mats:
        sums = jnp.sum(jnp.abs(mat), axis=0, keepdims=True)
        over = 1.0 / (jnp.max(sums, axis=1, keepdims=True) * 1.0001)
        low = lowest * over
        start = over * mat
        factor = factor_of(start, low)
        starts.append(start)
        overs.append(over)
        factors.append(factor)
        lows.append(raised(low))
    products = [three_pass(start, factor) for start, factor in zip(starts, factors)]
    found = [over * factor for over, factor in zip(overs, factors)]
    for _ in range(carried):
        factors = [factor_of(product, low) for product, low in zip(products, lows)]
        found = [three_pass(x, factor) for x, factor in zip(found, factors)]
        products = [three_pass(product, factor) for product, factor in zip(products, factors)]
        lows = [raised(low) for low in lows]
    products = [three_pass(mat, x) for mat, x in zip(mats, found)]
    found = [three_pass(x, factor_of(product, low)) for x, product, low in zip(found, products, lows)]
    if not last:
        return found
    lows = [raised(low) for low in lows]
    products = [three_pass(mat, x) for mat, x in zip(mats, found)]
    return [
        x + three_pass(x, factor_of(product, low) - eye) for x, product, low in zip(found, products, lows)
    ]


def kernel(
    n_band, n_reg, slots,
    values_hbm, coords_hbm, near_hbm, params_hbm,
    grad_ref, theta_ref,
    values_ref, coords_ref, near_ref, params_ref,
    ask_out, ask_in, rows_out, rows_in, back_out, back_in,
    rimplace_in, rim_in, rimback_out, rimback_in,
    th_out, th_in, tb_out, tb_in,
    chosen_ref, spread_ref, sel_ref, kern_ref, shape_ref, slope_ref,
    local_sems, send_sems, recv_sems, known_sems,
):
    band, reg = lax.axis_index("band"), lax.axis_index("region")
    points, reps = values_ref.shape
    blocks, width = near_ref.shape
    length = points // blocks
    half = points // 2
    order_n = width + length
    rim_start = points - RIM

    def turned(k, n):
        by = (k + 1) // 2
        return lax.rem(n // 2 + jnp.where(lax.rem(k, 2) == 0, by, n - by), n)

    side = 1
    while 2 * (2 * side) ** 2 <= n_reg:
        side *= 2
    tall = n_reg // (2 * side)

    def region_peer(i):
        k = i - 1
        y, x, core = reg // (2 * side), lax.rem(reg // 2, side), lax.rem(reg, 2)
        y = lax.rem(y + turned(k // (2 * side), tall), tall)
        x = lax.rem(x + turned(lax.rem(k // 2, side), side), side)
        core = lax.rem(core + 1 + lax.rem(k, 2), 2)
        return (y * side + x) * 2 + core

    def band_peer(i):
        return lax.rem(band + i, n_band)

    arrivals = [
        pltpu.make_async_copy(source, target, local_sems.at[k])
        for k, (source, target) in enumerate(
            [(coords_hbm, coords_ref), (near_hbm, near_ref), (values_hbm, values_ref), (params_hbm, params_ref)]
        )
    ]
    for copy in arrivals:
        copy.start()

    barrier = pltpu.get_barrier_semaphore()

    def greet_region(i, c):
        pl.semaphore_signal(barrier, inc=1, device_id=(band, region_peer(i)), device_id_type=MESH)
        return c

    for i in (1, n_band - 1):
        pl.semaphore_signal(barrier, inc=1, device_id=(band_peer(i), reg), device_id_type=MESH)
    lax.fori_loop(1, n_reg, greet_region, 0, unroll=True)

    rounds = []
    while 2 ** (len(rounds) + 1) <= n_band // 2:
        rounds.append(2 ** len(rounds))

    def tell(k):
        for side, by in enumerate((rounds[k], n_band - rounds[k])):
            pl.semaphore_signal(
                known_sems.at[k, side], inc=1, device_id=(band_peer(by), reg), device_id_type=MESH
            )

    def hear(k):
        for side in range(2):
            pl.semaphore_wait(known_sems.at[k, side], 1)

    def to_peers(source, into, stage):
        def send(i, c):
            peer = region_peer(i)
            pltpu.make_async_remote_copy(
                src_ref=source(peer), dst_ref=into.at[reg],
                send_sem=send_sems.at[stage], recv_sem=recv_sems.at[stage],
                device_id=(band, peer), device_id_type=MESH,
            ).start()
            return c
        lax.fori_loop(1, n_reg, send, 0, unroll=True)

    def from_peers(into, stage):
        some = pl.ds(0, n_reg - 1)
        return pltpu.make_async_remote_copy(
            src_ref=into.at[some], dst_ref=into.at[some],
            send_sem=send_sems.at[stage], recv_sem=recv_sems.at[stage],
            device_id=(band, region_peer(1)), device_id_type=MESH,
        )

    def up_band(source, into, stage, by):
        return pltpu.make_async_remote_copy(
            src_ref=source, dst_ref=into, send_sem=send_sems.at[stage], recv_sem=recv_sems.at[stage],
            device_id=(band_peer(by), reg), device_id_type=MESH,
        )

    arrivals[1].wait()
    near = near_ref[...]
    owner = near // points
    offset = near - owner * points
    owner_band = owner // n_reg
    owner_reg = owner - owner_band * n_reg
    is_rim = owner_band == band - 1
    is_own = jnp.logical_and(owner_band == band, owner_reg == reg)
    is_far = jnp.logical_and(owner_band == band, owner_reg != reg)
    far_row = jnp.where(is_far, owner_reg, -1)
    table_row = jnp.where(is_rim, n_reg, owner_reg)
    off_t = [(iota((points, width), 0) == offset[b : b + 1]).astype(BF16) for b in range(blocks)]
    far_t = [(iota((n_reg, width), 0) == far_row[b : b + 1]).astype(F32) for b in range(blocks)]
    counts = sum(nt(far_t[b].astype(BF16), off_t[b]) for b in range(blocks))
    mask = (counts > 0.5).astype(F32)
    below = (iota((points, points), 0) < iota((points, points), 1)).astype(BF16)
    rank = nn(mask.astype(BF16), below)
    arrivals[0].wait()
    ask_out[:, 0, :] = jnp.broadcast_to(coords_ref[0:1, :], (n_reg, points))
    ask_out[:, 1, :] = jnp.broadcast_to(coords_ref[1:2, :], (n_reg, points))
    ask_out[:, 2, :] = mask
    ask_out[:, 3, :] = jnp.zeros((n_reg, points), F32)

    pl.semaphore_wait(barrier, n_reg + 1)
    rimplace_copy = up_band(coords_ref.at[:, pl.ds(half, half)], rimplace_in, 7, 1)
    rimplace_copy.start()
    to_peers(lambda peer: ask_out.at[peer], ask_in, 1)
    if rounds:
        tell(0)
    arrivals[2].wait()
    rim_copy = up_band(values_ref.at[pl.ds(rim_start, RIM)], rim_in, 4, 1)
    rim_copy.start()
    ask_in[pl.ds(reg, 1)] = ask_out[pl.ds(reg, 1)]
    rows_in[pl.ds(reg, 1)] = jnp.zeros((1, slots, reps), F32)
    back_in[pl.ds(reg, 1)] = jnp.zeros((1, slots, reps), F32)

    rank_bf = rank.astype(BF16)
    index_rows = []
    for b in range(blocks):
        slot = jnp.sum(far_t[b] * nn(rank_bf, off_t[b]), axis=0, keepdims=True).astype(jnp.int32)
        far_index = points + RIM + owner_reg[b : b + 1] * slots + slot
        rim_index = points + offset[b : b + 1] - rim_start
        index_rows.append(
            jnp.where(is_own[b : b + 1], offset[b : b + 1], jnp.where(is_rim[b : b + 1], rim_index, far_index))
        )
    table = chosen_ref.shape[2]
    index_cols = jnp.concatenate(index_rows + [jnp.zeros((8 - blocks, width), jnp.int32)], axis=0).astype(F32).T
    for b in range(blocks):
        column = index_cols[:, b : b + 1].astype(jnp.int32)
        chosen_ref[b] = (iota((width, table), 1) == column).astype(BF16)
        spread_ref[b] = (iota((table, width), 0) == index_rows[b]).astype(BF16)

    arrivals[3].wait()
    from_peers(ask_in, 1).wait_recv()
    rimplace_copy.wait_recv()

    x_row, y_row = coords_ref[0:1, :], coords_ref[1:2, :]
    zero_half = jnp.zeros((1, half), F32)
    tables = []
    for k in range(2):
        rim_row = jnp.concatenate([zero_half, rimplace_in[k : k + 1, :]], axis=1)
        tables += [ask_in[:, k, :], rim_row, jnp.zeros((7, points), F32)]
    coord_table = jnp.concatenate(tables, axis=0)
    rows = n_reg + 8
    variance = jnp.exp(jnp.full((1, 1), params_ref[0], F32))
    inverse_range = jnp.sqrt(jnp.full((1, 1), 3.0, F32)) * jnp.exp(jnp.full((1, 1), -params_ref[1], F32))
    nugget = jnp.exp(jnp.full((1, 1), params_ref[2], F32))
    parts = split(coord_table, 3)
    for b in range(blocks):
        own_t = (iota((rows, width), 0) == table_row[b : b + 1]).astype(F32)
        found = sum(nn(part, off_t[b]) for part in reversed(parts))
        x_near = jnp.sum(own_t * found[:rows], axis=0, keepdims=True)
        y_near = jnp.sum(own_t * found[rows:], axis=0, keepdims=True)
        here = slice(b * length, (b + 1) * length)
        x_joint = jnp.concatenate([x_near, x_row[:, here]], axis=1)
        y_joint = jnp.concatenate([y_near, y_row[:, here]], axis=1)
        cols = jnp.concatenate([x_joint, y_joint, jnp.zeros((6, order_n), F32)], axis=0).T
        delta_x = cols[:, 0:1] - x_joint
        delta_y = cols[:, 1:2] - y_joint
        scaled = inverse_range * jnp.sqrt(delta_x * delta_x + delta_y * delta_y)
        decayed = variance * jnp.exp(-scaled)
        shape_part = decayed + scaled * decayed
        shape_ref[b] = shape_part
        slope_ref[b] = scaled * scaled * decayed
        diagonal = iota((order_n, order_n), 0) == iota((order_n, order_n), 1)
        kern_ref[b] = jnp.where(diagonal, shape_part + nugget, shape_part)

    wanted = ask_in[:, 2, :]
    wanted_rank = nn(wanted.astype(BF16), below)
    slot_of = jnp.where(wanted > 0.5, wanted_rank, -1.0)
    sel = (
        jnp.broadcast_to(slot_of[:, None, :], (n_reg, slots, points))
        == iota((n_reg, slots, points), 1).astype(F32)
    )
    sel_ref[...] = sel.astype(F32).reshape(n_reg * slots, points).astype(BF16)
    rows_out[...] = picked(nn, sel_ref[...], values_ref[...]).reshape(n_reg, slots, reps)
    to_peers(lambda peer: rows_out.at[peer], rows_in, 2)

    if len(rounds) > 1:
        hear(0)
        tell(1)
    all_blocks = range(blocks)
    inv_a = inverses([kern_ref[b, :width, :width] for b in all_blocks], nugget, 5, False)
    x_t = [three_pass(kern_ref[b, width:, :width], inv_a[b]) for b in all_blocks]
    missed = [kern_ref[b, width:, :width] - three_pass(x_t[b], kern_ref[b, :width, :width]) for b in all_blocks]
    x_t = [x_t[b] + three_pass(missed[b], inv_a[b]) for b in all_blocks]
    x_n = [x.T for x in x_t]
    schur = [kern_ref[b, width:, width:] - three_pass(x_t[b], kern_ref[b, :width, width:]) for b in all_blocks]
    inv_s = inverses(schur, nugget, 4, True)

    if len(rounds) > 2:
        hear(1)
        tell(2)
    rim_copy.wait_recv()
    from_peers(rows_in, 2).wait_recv()
    pad = table - points - RIM - n_reg * slots
    value_table = jnp.concatenate(
        [values_ref[...], rim_in[...], rows_in[...].reshape(n_reg * slots, reps), jnp.zeros((pad, reps), F32)],
        axis=0,
    )
    near_rows = [picked(nn, chosen_ref[b], value_table) for b in all_blocks]
    own_rows = [values_ref[b * length : (b + 1) * length, :] for b in all_blocks]
    resids = [own_rows[b] - three_pass(x_t[b], near_rows[b]) for b in all_blocks]
    heads = [three_pass(inv_a[b], near_rows[b]) for b in all_blocks]
    missed = [near_rows[b] - three_pass(kern_ref[b, :width, :width], heads[b]) for b in all_blocks]
    heads = [heads[b] + three_pass(inv_a[b], missed[b]) for b in all_blocks]
    us = [three_pass(inv_s[b], resids[b]) for b in all_blocks]
    backs = [three_pass(x_n[b], us[b]) for b in all_blocks]

    sums = [jnp.zeros((1, 1), F32)] * 3
    for b in all_blocks:
        u, head_back = us[b], -backs[b]
        back = jnp.concatenate([head_back, u], axis=0)
        left = jnp.concatenate([heads[b] + 0.5 * head_back, 0.5 * u], axis=0)
        v = jnp.concatenate(
            [-x_n[b], (iota((length, length), 0) == iota((length, length), 1)).astype(F32)], axis=0
        )
        vs = (-0.5 * reps) * jnp.concatenate([-three_pass(x_n[b], inv_s[b]), inv_s[b]], axis=0)
        left = jnp.concatenate([left, vs], axis=1)
        right = jnp.concatenate([back, v], axis=1)
        grad_kernel = three_pass(left, right, nt)
        total = lambda z: jnp.sum(jnp.sum(z, axis=0, keepdims=True), axis=1, keepdims=True)
        sums = [
            sums[0] + total(grad_kernel * shape_ref[b]),
            sums[1] + total(grad_kernel * slope_ref[b]),
            sums[2] + nugget * total(left * right),
        ]
    lane = iota((1, half), 1)
    mine = jnp.where(lane == 0, sums[0], jnp.where(lane == 1, sums[1], jnp.where(lane == 2, sums[2], 0.0)))
    th_out[...] = mine
    to_peers(lambda peer: th_out, th_in, 5)
    th_in[pl.ds(reg, 1)] = mine[None]

    spread = sum(picked(nn, spread_ref[b], backs[b]) for b in all_blocks)
    back_out[...] = spread[points + RIM : points + RIM + n_reg * slots].reshape(n_reg, slots, reps)
    rimback_out[...] = spread[points : points + RIM]
    grad_ref[...] = spread[:points] - jnp.concatenate(us, axis=0)
    if rounds:
        hear(len(rounds) - 1)
    from_peers(th_in, 5).wait_recv()
    band_sum = jnp.sum(th_in[...], axis=0)
    tb_out[...] = band_sum

    def send_band(i, c):
        pltpu.make_async_remote_copy(
            src_ref=tb_out, dst_ref=tb_in.at[band], send_sem=send_sems.at[6], recv_sem=recv_sems.at[6],
            device_id=(band_peer(i), reg), device_id_type=MESH,
        ).start()
        return c

    lax.fori_loop(0, n_band - 1, lambda k, c: send_band(turned(k, n_band), c), 0, unroll=True)
    tb_in[pl.ds(band, 1)] = band_sum[None]
    to_peers(lambda peer: back_out.at[peer], back_in, 3)
    rimback_copy = up_band(rimback_out, rimback_in, 8, n_band - 1)
    rimback_copy.start()

    rimback_copy.wait_recv()
    from_peers(back_in, 3).wait_recv()
    returned = back_in[...].reshape(n_reg * slots, reps)
    grad_ref[...] += picked(tn, sel_ref[...], returned)
    grad_ref[rim_start:, :] += rimback_in[...]

    from_bands = pltpu.make_async_remote_copy(
        src_ref=tb_in.at[pl.ds(0, n_band - 1)], dst_ref=tb_in.at[pl.ds(0, n_band - 1)],
        send_sem=send_sems.at[6], recv_sem=recv_sems.at[6],
        device_id=(band_peer(1), reg), device_id_type=MESH,
    )
    from_bands.wait_recv()
    theta_ref[...] = jnp.sum(tb_in[...], axis=0) * (1.0 / (points * n_band * n_reg * reps))

    from_peers(ask_in, 1).wait_send()
    from_peers(rows_in, 2).wait_send()
    from_peers(back_in, 3).wait_send()
    from_peers(th_in, 5).wait_send()
    from_bands.wait_send()
    rimplace_copy.wait_send()
    rim_copy.wait_send()
    rimback_copy.wait_send()


def shards(n_band, n_reg, values, coords, neighbours, log_params):
    points, reps = values.shape
    blocks, width = neighbours.shape
    length = points // blocks
    order_n = width + length
    cap = (2 * POOL + n_reg - 2) // (n_reg - 1)
    slots = -(-cap // 16) * 16
    table = -(-(points + RIM + n_reg * slots) // 128) * 128
    half = points // 2
    vmem = lambda *shape: pltpu.VMEM(shape, F32)
    grad, theta = pl.pallas_call(
        functools.partial(kernel, n_band, n_reg, slots),
        out_shape=(pltpu.VMEM((points, reps), F32), pltpu.VMEM((1, half), F32)),
        in_specs=[pl.BlockSpec(memory_space=pltpu.HBM)] * 4,
        out_specs=(pl.BlockSpec(memory_space=pltpu.VMEM), pl.BlockSpec(memory_space=pltpu.VMEM)),
        scratch_shapes=[
            vmem(points, reps), vmem(2, points), pltpu.VMEM((blocks, width), jnp.int32),
            pltpu.SMEM((3,), F32),
            vmem(n_reg, 4, points), vmem(n_reg, 4, points),
            vmem(n_reg, slots, reps), vmem(n_reg, slots, reps),
            vmem(n_reg, slots, reps), vmem(n_reg, slots, reps),
            vmem(2, half), vmem(RIM, reps), vmem(RIM, reps), vmem(RIM, reps),
            vmem(1, half), vmem(n_reg, 1, half), vmem(1, half), vmem(n_band, 1, half),
            pltpu.VMEM((blocks, width, table), BF16), pltpu.VMEM((blocks, table, width), BF16),
            pltpu.VMEM((n_reg * slots, points), BF16),
            vmem(blocks, order_n, order_n), vmem(blocks, order_n, order_n), vmem(blocks, order_n, order_n),
            pltpu.SemaphoreType.DMA((4,)), pltpu.SemaphoreType.DMA((9,)), pltpu.SemaphoreType.DMA((9,)),
            pltpu.SemaphoreType.REGULAR((4, 2)),
        ],
        compiler_params=pltpu.CompilerParams(
            collective_id=0, has_side_effects=True, vmem_limit_bytes=60 * 1024 * 1024
        ),
    )(values, coords, neighbours, log_params)
    return grad, theta[0, :3]


def solution(mesh):
    placed = (
        P(("band", "region"), None),
        P(None, ("band", "region")),
        P(("band", "region"), None),
        P(),
    )
    return jax.shard_map(
        functools.partial(shards, mesh.shape["band"], mesh.shape["region"]),
        mesh=mesh,
        in_specs=placed,
        out_specs=(P(("band", "region"), None), P()),
        check_vma=False,
    )
```

```python
import functools

import jax
import jax.numpy as jnp
from jax import lax
from jax.experimental import pallas as pl
from jax.experimental.pallas import tpu as pltpu
from jax.sharding import PartitionSpec as P

MESH = pl.DeviceIdType.MESH
F32 = jnp.float32
BF16 = jnp.bfloat16
M = 256
RIM = 64
POOL = 160


def split(x, parts):
    out = []
    for _ in range(parts - 1):
        high = x.astype(BF16)
        out.append(high)
        x = x - high.astype(F32)
    out.append(x.astype(BF16))
    return out


def nn(a, b):
    return lax.dot_general(a, b, (((1,), (0,)), ((), ())), preferred_element_type=F32)


def nt(a, b):
    return lax.dot_general(a, b, (((1,), (1,)), ((), ())), preferred_element_type=F32)


def tn(a, b):
    return lax.dot_general(a, b, (((0,), (0,)), ((), ())), preferred_element_type=F32)


def three_pass(a, b, dot=nn):
    a_high, a_low = split(a, 2)
    b_high, b_low = split(b, 2)
    n = b.shape[1]
    if dot is nn and n <= 128:
        wide = jnp.concatenate([b_high, b_low], axis=1)
        if a.shape[1] <= 128:
            both = nn(jnp.concatenate([a_high, a_low], axis=1), jnp.concatenate([wide, wide], axis=0))
            return both[:, :n] + both[:, n:]
        both = nn(a_high, wide)
        return both[:, :n] + (both[:, n:] + nn(a_low, b_high))
    return dot(a_high, b_high) + (dot(a_high, b_low) + dot(a_low, b_high))


def picked(dot, chosen, x):
    n = x.shape[1]
    both = dot(chosen, jnp.concatenate(split(x, 2), axis=1))
    return both[:, :n] + both[:, n:]


def iota(shape, dim):
    return lax.broadcasted_iota(jnp.int32, shape, dim)


def inverses(mats, lowest, carried, last):
    n = mats[0].shape[0]
    eye = (iota((n, n), 0) == iota((n, n), 1)).astype(F32)

    def factor_of(product, low):
        scale = 2.0 / (1.0 + low)
        return (2.0 * scale) * eye - (scale * scale) * product

    def raised(low):
        return 4.0 * low / ((1.0 + low) * (1.0 + low))

    lows, overs, factors, starts = [], [], [], []
    for mat in mats:
        sums = jnp.sum(jnp.abs(mat), axis=0, keepdims=True)
        over = 1.0 / (jnp.max(sums, axis=1, keepdims=True) * 1.0001)
        low = lowest * over
        start = over * mat
        factor = factor_of(start, low)
        starts.append(start)
        overs.append(over)
        factors.append(factor)
        lows.append(raised(low))
    products = [three_pass(start, factor) for start, factor in zip(starts, factors)]
    found = [over * factor for over, factor in zip(overs, factors)]
    for _ in range(carried):
        factors = [factor_of(product, low) for product, low in zip(products, lows)]
        found = [three_pass(x, factor) for x, factor in zip(found, factors)]
        products = [three_pass(product, factor) for product, factor in zip(products, factors)]
        lows = [raised(low) for low in lows]
    products = [three_pass(mat, x) for mat, x in zip(mats, found)]
    found = [three_pass(x, factor_of(product, low)) for x, product, low in zip(found, products, lows)]
    if not last:
        return found
    lows = [raised(low) for low in lows]
    products = [three_pass(mat, x) for mat, x in zip(mats, found)]
    return [
        x + three_pass(x, factor_of(product, low) - eye) for x, product, low in zip(found, products, lows)
    ]


def kernel(
    n_band, n_reg, slots,
    values_hbm, coords_hbm, near_hbm, params_hbm,
    grad_ref, theta_ref,
    values_ref, coords_ref, near_ref, params_ref,
    ask_out, ask_in, rows_out, rows_in, back_out, back_in,
    rimplace_in, rim_in, rimback_out, rimback_in,
    th_out, th_in, tb_out, tb_in,
    chosen_ref, spread_ref, sel_ref, kern_ref, shape_ref, slope_ref,
    local_sems, send_sems, recv_sems, known_sems,
):
    band, reg = lax.axis_index("band"), lax.axis_index("region")
    points, reps = values_ref.shape
    blocks, width = near_ref.shape
    length = points // blocks
    half = points // 2
    order_n = width + length
    rim_start = points - RIM

    def turned(k, n):
        by = (k + 1) // 2
        return lax.rem(n // 2 + jnp.where(lax.rem(k, 2) == 0, by, n - by), n)

    side = 1
    while 2 * (2 * side) ** 2 <= n_reg:
        side *= 2
    tall = n_reg // (2 * side)

    def region_peer(i):
        k = i - 1
        y, x, core = reg // (2 * side), lax.rem(reg // 2, side), lax.rem(reg, 2)
        y = lax.rem(y + turned(k // (2 * side), tall), tall)
        x = lax.rem(x + turned(lax.rem(k // 2, side), side), side)
        core = lax.rem(core + 1 + lax.rem(k, 2), 2)
        return (y * side + x) * 2 + core

    def band_peer(i):
        return lax.rem(band + i, n_band)

    arrivals = [
        pltpu.make_async_copy(source, target, local_sems.at[k])
        for k, (source, target) in enumerate(
            [(coords_hbm, coords_ref), (near_hbm, near_ref), (values_hbm, values_ref), (params_hbm, params_ref)]
        )
    ]
    for copy in arrivals:
        copy.start()

    barrier = pltpu.get_barrier_semaphore()

    def greet_region(i, c):
        pl.semaphore_signal(barrier, inc=1, device_id=(band, region_peer(i)), device_id_type=MESH)
        return c

    for i in (1, n_band - 1):
        pl.semaphore_signal(barrier, inc=1, device_id=(band_peer(i), reg), device_id_type=MESH)
    lax.fori_loop(1, n_reg, greet_region, 0, unroll=True)

    rounds = []
    while 2 ** (len(rounds) + 1) <= n_band // 2:
        rounds.append(2 ** len(rounds))

    def tell(k):
        for side, by in enumerate((rounds[k], n_band - rounds[k])):
            pl.semaphore_signal(
                known_sems.at[k, side], inc=1, device_id=(band_peer(by), reg), device_id_type=MESH
            )

    def hear(k):
        for side in range(2):
            pl.semaphore_wait(known_sems.at[k, side], 1)

    def to_peers(source, into, stage):
        def send(i, c):
            peer = region_peer(i)
            pltpu.make_async_remote_copy(
                src_ref=source(peer), dst_ref=into.at[reg],
                send_sem=send_sems.at[stage], recv_sem=recv_sems.at[stage],
                device_id=(band, peer), device_id_type=MESH,
            ).start()
            return c
        lax.fori_loop(1, n_reg, send, 0, unroll=True)

    def from_peers(into, stage):
        some = pl.ds(0, n_reg - 1)
        return pltpu.make_async_remote_copy(
            src_ref=into.at[some], dst_ref=into.at[some],
            send_sem=send_sems.at[stage], recv_sem=recv_sems.at[stage],
            device_id=(band, region_peer(1)), device_id_type=MESH,
        )

    def up_band(source, into, stage, by):
        return pltpu.make_async_remote_copy(
            src_ref=source, dst_ref=into, send_sem=send_sems.at[stage], recv_sem=recv_sems.at[stage],
            device_id=(band_peer(by), reg), device_id_type=MESH,
        )

    arrivals[1].wait()
    near = near_ref[...]
    owner = near // points
    offset = near - owner * points
    owner_band = owner // n_reg
    owner_reg = owner - owner_band * n_reg
    is_rim = owner_band == band - 1
    is_own = jnp.logical_and(owner_band == band, owner_reg == reg)
    is_far = jnp.logical_and(owner_band == band, owner_reg != reg)
    far_row = jnp.where(is_far, owner_reg, -1)
    table_row = jnp.where(is_rim, n_reg, owner_reg)
    off_t = [(iota((points, width), 0) == offset[b : b + 1]).astype(BF16) for b in range(blocks)]
    far_t = [(iota((n_reg, width), 0) == far_row[b : b + 1]).astype(F32) for b in range(blocks)]
    counts = sum(nt(far_t[b].astype(BF16), off_t[b]) for b in range(blocks))
    mask = (counts > 0.5).astype(F32)
    below = (iota((points, points), 0) < iota((points, points), 1)).astype(BF16)
    rank = nn(mask.astype(BF16), below)
    arrivals[0].wait()
    ask_out[:, 0, :] = jnp.broadcast_to(coords_ref[0:1, :], (n_reg, points))
    ask_out[:, 1, :] = jnp.broadcast_to(coords_ref[1:2, :], (n_reg, points))
    ask_out[:, 2, :] = mask

    pl.semaphore_wait(barrier, n_reg + 1)
    rimplace_copy = up_band(coords_ref.at[:, pl.ds(half, half)], rimplace_in, 7, 1)
    rimplace_copy.start()
    to_peers(lambda peer: ask_out.at[peer], ask_in, 1)
    if rounds:
        tell(0)
    arrivals[2].wait()
    rim_copy = up_band(values_ref.at[pl.ds(rim_start, RIM)], rim_in, 4, 1)
    rim_copy.start()
    ask_in[pl.ds(reg, 1)] = ask_out[pl.ds(reg, 1)]
    rows_in[pl.ds(reg, 1)] = jnp.zeros((1, slots, reps), F32)
    back_in[pl.ds(reg, 1)] = jnp.zeros((1, slots, reps), F32)

    rank_bf = rank.astype(BF16)
    index_rows = []
    for b in range(blocks):
        slot = jnp.sum(far_t[b] * nn(rank_bf, off_t[b]), axis=0, keepdims=True).astype(jnp.int32)
        far_index = points + RIM + owner_reg[b : b + 1] * slots + slot
        rim_index = points + offset[b : b + 1] - rim_start
        index_rows.append(
            jnp.where(is_own[b : b + 1], offset[b : b + 1], jnp.where(is_rim[b : b + 1], rim_index, far_index))
        )
    table = chosen_ref.shape[2]
    index_cols = jnp.concatenate(index_rows + [jnp.zeros((8 - blocks, width), jnp.int32)], axis=0).astype(F32).T
    for b in range(blocks):
        column = index_cols[:, b : b + 1].astype(jnp.int32)
        chosen_ref[b] = (iota((width, table), 1) == column).astype(BF16)
        spread_ref[b] = (iota((table, width), 0) == index_rows[b]).astype(BF16)

    arrivals[3].wait()
    from_peers(ask_in, 1).wait_recv()
    rimplace_copy.wait_recv()

    x_row, y_row = coords_ref[0:1, :], coords_ref[1:2, :]
    zero_half = jnp.zeros((1, half), F32)
    tables = []
    for k in range(2):
        rim_row = jnp.concatenate([zero_half, rimplace_in[k : k + 1, :]], axis=1)
        tables += [ask_in[:, k, :], rim_row, jnp.zeros((7, points), F32)]
    coord_table = jnp.concatenate(tables, axis=0)
    rows = n_reg + 8
    variance = jnp.exp(jnp.full((1, 1), params_ref[0], F32))
    inverse_range = jnp.sqrt(jnp.full((1, 1), 3.0, F32)) * jnp.exp(jnp.full((1, 1), -params_ref[1], F32))
    nugget = jnp.exp(jnp.full((1, 1), params_ref[2], F32))
    parts = split(coord_table, 3)
    for b in range(blocks):
        own_t = (iota((rows, width), 0) == table_row[b : b + 1]).astype(F32)
        found = sum(nn(part, off_t[b]) for part in reversed(parts))
        x_near = jnp.sum(own_t * found[:rows], axis=0, keepdims=True)
        y_near = jnp.sum(own_t * found[rows:], axis=0, keepdims=True)
        here = slice(b * length, (b + 1) * length)
        x_joint = jnp.concatenate([x_near, x_row[:, here]], axis=1)
        y_joint = jnp.concatenate([y_near, y_row[:, here]], axis=1)
        cols = jnp.concatenate([x_joint, y_joint, jnp.zeros((6, order_n), F32)], axis=0).T
        delta_x = cols[:, 0:1] - x_joint
        delta_y = cols[:, 1:2] - y_joint
        scaled = inverse_range * jnp.sqrt(delta_x * delta_x + delta_y * delta_y)
        decayed = variance * jnp.exp(-scaled)
        shape_part = decayed + scaled * decayed
        shape_ref[b] = shape_part
        slope_ref[b] = scaled * scaled * decayed
        diagonal = iota((order_n, order_n), 0) == iota((order_n, order_n), 1)
        kern_ref[b] = jnp.where(diagonal, shape_part + nugget, shape_part)

    wanted = ask_in[:, 2, :]
    wanted_rank = nn(wanted.astype(BF16), below)
    slot_of = jnp.where(wanted > 0.5, wanted_rank, -1.0)
    sel = (
        jnp.broadcast_to(slot_of[:, None, :], (n_reg, slots, points))
        == iota((n_reg, slots, points), 1).astype(F32)
    )
    sel_ref[...] = sel.astype(F32).reshape(n_reg * slots, points).astype(BF16)
    rows_out[...] = picked(nn, sel_ref[...], values_ref[...]).reshape(n_reg, slots, reps)
    to_peers(lambda peer: rows_out.at[peer], rows_in, 2)

    if len(rounds) > 1:
        hear(0)
        tell(1)
    all_blocks = range(blocks)
    inv_a = inverses([kern_ref[b, :width, :width] for b in all_blocks], nugget, 5, False)
    x_t = [three_pass(kern_ref[b, width:, :width], inv_a[b]) for b in all_blocks]
    missed = [kern_ref[b, width:, :width] - three_pass(x_t[b], kern_ref[b, :width, :width]) for b in all_blocks]
    x_t = [x_t[b] + three_pass(missed[b], inv_a[b]) for b in all_blocks]
    x_n = [x.T for x in x_t]
    schur = [kern_ref[b, width:, width:] - three_pass(x_t[b], kern_ref[b, :width, width:]) for b in all_blocks]
    inv_s = inverses(schur, nugget, 4, True)

    one = (iota((length, length), 0) == iota((length, length), 1)).astype(F32)
    v = [jnp.concatenate([-x_n[b], one], axis=0) for b in all_blocks]
    vs = [
        (-0.5 * reps) * jnp.concatenate([-three_pass(x_n[b], inv_s[b]), inv_s[b]], axis=0) for b in all_blocks
    ]

    if len(rounds) > 2:
        hear(1)
        tell(2)
    rim_copy.wait_recv()
    from_peers(rows_in, 2).wait_recv()
    pad = table - points - RIM - n_reg * slots
    value_table = jnp.concatenate(
        [values_ref[...], rim_in[...], rows_in[...].reshape(n_reg * slots, reps), jnp.zeros((pad, reps), F32)],
        axis=0,
    )
    near_rows = [picked(nn, chosen_ref[b], value_table) for b in all_blocks]
    own_rows = [values_ref[b * length : (b + 1) * length, :] for b in all_blocks]
    resids = [own_rows[b] - three_pass(x_t[b], near_rows[b]) for b in all_blocks]
    heads = [three_pass(inv_a[b], near_rows[b]) for b in all_blocks]
    missed = [near_rows[b] - three_pass(kern_ref[b, :width, :width], heads[b]) for b in all_blocks]
    heads = [heads[b] + three_pass(inv_a[b], missed[b]) for b in all_blocks]
    us = [three_pass(inv_s[b], resids[b]) for b in all_blocks]
    backs = [three_pass(x_n[b], us[b]) for b in all_blocks]

    sums = [jnp.zeros((1, 1), F32)] * 3
    for b in all_blocks:
        u, head_back = us[b], -backs[b]
        back = jnp.concatenate([head_back, u], axis=0)
        left = jnp.concatenate([heads[b] + 0.5 * head_back, 0.5 * u], axis=0)
        left = jnp.concatenate([left, vs[b]], axis=1)
        right = jnp.concatenate([back, v[b]], axis=1)
        grad_kernel = three_pass(left, right, nt)
        total = lambda z: jnp.sum(jnp.sum(z, axis=0, keepdims=True), axis=1, keepdims=True)
        sums = [
            sums[0] + total(grad_kernel * shape_ref[b]),
            sums[1] + total(grad_kernel * slope_ref[b]),
            sums[2] + nugget * total(left * right),
        ]
    lane = iota((1, half), 1)
    mine = jnp.where(lane == 0, sums[0], jnp.where(lane == 1, sums[1], jnp.where(lane == 2, sums[2], 0.0)))
    th_out[...] = mine
    to_peers(lambda peer: th_out, th_in, 5)
    th_in[pl.ds(reg, 1)] = mine[None]

    spread = sum(picked(nn, spread_ref[b], backs[b]) for b in all_blocks)
    back_out[...] = spread[points + RIM : points + RIM + n_reg * slots].reshape(n_reg, slots, reps)
    rimback_out[...] = spread[points : points + RIM]
    grad_ref[...] = spread[:points] - jnp.concatenate(us, axis=0)
    if rounds:
        hear(len(rounds) - 1)
    from_peers(th_in, 5).wait_recv()
    band_sum = jnp.sum(th_in[...], axis=0)
    tb_out[...] = band_sum

    def send_band(i, c):
        pltpu.make_async_remote_copy(
            src_ref=tb_out, dst_ref=tb_in.at[band], send_sem=send_sems.at[6], recv_sem=recv_sems.at[6],
            device_id=(band_peer(i), reg), device_id_type=MESH,
        ).start()
        return c

    lax.fori_loop(0, n_band - 1, lambda k, c: send_band(turned(k, n_band), c), 0, unroll=True)
    tb_in[pl.ds(band, 1)] = band_sum[None]
    to_peers(lambda peer: back_out.at[peer], back_in, 3)
    rimback_copy = up_band(rimback_out, rimback_in, 8, n_band - 1)
    rimback_copy.start()

    rimback_copy.wait_recv()
    from_peers(back_in, 3).wait_recv()
    returned = back_in[...].reshape(n_reg * slots, reps)
    grad_ref[...] += picked(tn, sel_ref[...], returned)
    grad_ref[rim_start:, :] += rimback_in[...]

    from_bands = pltpu.make_async_remote_copy(
        src_ref=tb_in.at[pl.ds(0, n_band - 1)], dst_ref=tb_in.at[pl.ds(0, n_band - 1)],
        send_sem=send_sems.at[6], recv_sem=recv_sems.at[6],
        device_id=(band_peer(1), reg), device_id_type=MESH,
    )
    from_bands.wait_recv()
    theta_ref[...] = jnp.sum(tb_in[...], axis=0) * (1.0 / (points * n_band * n_reg * reps))

    from_peers(ask_in, 1).wait_send()
    from_peers(rows_in, 2).wait_send()
    from_peers(back_in, 3).wait_send()
    from_peers(th_in, 5).wait_send()
    from_bands.wait_send()
    rimplace_copy.wait_send()
    rim_copy.wait_send()
    rimback_copy.wait_send()


def shards(n_band, n_reg, values, coords, neighbours, log_params):
    points, reps = values.shape
    blocks, width = neighbours.shape
    length = points // blocks
    order_n = width + length
    cap = (2 * POOL + n_reg - 2) // (n_reg - 1)
    slots = -(-cap // 16) * 16
    table = -(-(points + RIM + n_reg * slots) // 128) * 128
    half = points // 2
    vmem = lambda *shape: pltpu.VMEM(shape, F32)
    grad, theta = pl.pallas_call(
        functools.partial(kernel, n_band, n_reg, slots),
        out_shape=(pltpu.VMEM((points, reps), F32), pltpu.VMEM((1, half), F32)),
        in_specs=[pl.BlockSpec(memory_space=pltpu.HBM)] * 4,
        out_specs=(pl.BlockSpec(memory_space=pltpu.VMEM), pl.BlockSpec(memory_space=pltpu.VMEM)),
        scratch_shapes=[
            vmem(points, reps), vmem(2, points), pltpu.VMEM((blocks, width), jnp.int32),
            pltpu.SMEM((3,), F32),
            vmem(n_reg, 3, points), vmem(n_reg, 3, points),
            vmem(n_reg, slots, reps), vmem(n_reg, slots, reps),
            vmem(n_reg, slots, reps), vmem(n_reg, slots, reps),
            vmem(2, half), vmem(RIM, reps), vmem(RIM, reps), vmem(RIM, reps),
            vmem(1, half), vmem(n_reg, 1, half), vmem(1, half), vmem(n_band, 1, half),
            pltpu.VMEM((blocks, width, table), BF16), pltpu.VMEM((blocks, table, width), BF16),
            pltpu.VMEM((n_reg * slots, points), BF16),
            vmem(blocks, order_n, order_n), vmem(blocks, order_n, order_n), vmem(blocks, order_n, order_n),
            pltpu.SemaphoreType.DMA((4,)), pltpu.SemaphoreType.DMA((9,)), pltpu.SemaphoreType.DMA((9,)),
            pltpu.SemaphoreType.REGULAR((4, 2)),
        ],
        compiler_params=pltpu.CompilerParams(
            collective_id=0, has_side_effects=True, vmem_limit_bytes=60 * 1024 * 1024
        ),
    )(values, coords, neighbours, log_params)
    return grad, theta[0, :3]


def solution(mesh):
    placed = (
        P(("band", "region"), None),
        P(None, ("band", "region")),
        P(("band", "region"), None),
        P(),
    )
    return jax.shard_map(
        functools.partial(shards, mesh.shape["band"], mesh.shape["region"]),
        mesh=mesh,
        in_specs=placed,
        out_specs=(P(("band", "region"), None), P()),
        check_vma=False,
    )
```
